512 devices in a mesh: rows: 64 (over x, z_lo, y), grp: 8 (over z_hi, core).
Axes of the slice: x: 4, y: 4, z: 16 (z_hi: 4, z_lo: 4; z = z_hi * 4 + z_lo), core: 2. Of those that a mesh axis runs over, the one named last changes fastest.
Arguments:
- latent_features: bfloat16 [8, 96, 5, 128, 128], P('grp', None, None, 'rows'), may hold values from -6 to 6
- conv_weight: bfloat16 [27, 96, 96], replicated, may hold values from -0.125 to 0.125
- conv_bias: float32 [96], replicated, may hold values from -3 to 3
- out_weight: bfloat16 [27, 96, 3], replicated, may hold values from -0.125 to 0.125
- out_bias: float32 [3], replicated, may hold values from -3 to 3
- target_frames: bfloat16 [8, 3, 5, 128, 128], P('grp', None, None, 'rows'), may hold values from -96 to 96
Outputs:
- decoded: bfloat16 [8, 3, 5, 128, 128], P('grp', None, None, 'rows')
- grad_conv_weight: float32 [27, 96, 96], replicated
- grad_conv_bias: float32 [96], replicated
- grad_out_weight: float32 [27, 96, 3], replicated
- grad_out_bias: float32 [3], replicated
The draws below stay inside these ranges and needn't reach their ends.
All inputs are finite; a program needn't handle non-finite values.
Results may differ from the reference program's by a relative error of at most 0.005.
Values may be sent and summed in bfloat16 or wider, within the bound.
No kernel may reach another device: no remote copies, remote signals or barrier semaphores. Data moves between devices by JAX's collectives and lax.ppermute only.
A program may use at most 64 MiB of HBM per device.

```python
import math
import jax
import jax.numpy as jnp
from jax import lax

C = 96
F = 5
ROWS_DEV = 2
W = 128
H = 128
CLIPS = 8


def draw_target_frames(key, part):
    key = jax.random.fold_in(key, 11)
    base_key = jax.random.fold_in(key, 1)
    offset_key = jax.random.fold_in(key, 2)
    shape = (CLIPS, 3, F, H, W)
    base = jnp.clip(jax.random.normal(base_key, shape, jnp.float32), -6.0, 6.0)
    clip_index = lax.broadcasted_iota(jnp.int32, shape, 0)
    row_index = lax.broadcasted_iota(jnp.int32, shape, 3)
    slab_index = clip_index * (H // ROWS_DEV) + row_index // ROWS_DEV
    offset = jax.random.randint(offset_key, (), 0, 32)
    heavy = (slab_index + offset) % 32 == 0
    factor = jnp.where(heavy, 16.0, 1.0).astype(jnp.float32)
    return (base * factor).astype(jnp.bfloat16)


def block_levels(key, extent, cuts, least, high):
    def one(position, parts):
        heights = jax.random.uniform(jax.random.fold_in(jax.random.fold_in(key, 6), position), (parts,), jnp.float32, least / len(cuts), high / len(cuts))
        return jnp.repeat(jnp.exp(heights), extent[position] // parts).reshape((-1,) + (1,) * (len(extent) - position - 1))

    gain = one(*cuts[0])
    for cut in cuts[1:]:
        gain = gain * one(*cut)
    return gain


def noise(own_key, shape, spread, limit, cuts=(), kind=jnp.bfloat16):
    gain = block_levels(own_key, shape, cuts, -0.22, 0.18) if cuts else 1.0
    values = jax.random.normal(own_key, shape, jnp.float32) * spread * gain
    return jnp.minimum(jnp.maximum(values, -limit), limit).astype(kind)


def setup_inputs(seed: int = 0) -> dict:
    seeds = jax.random.split(jax.random.key(seed), 7)
    latent_features = noise(seeds[0], (CLIPS, C, F, H, W), 1.0, 6.0, ((0, 8), (3, 64)))
    conv_weight = noise(seeds[1], (27, C, C), (27 * C) ** -0.5, 0.125)
    conv_bias = noise(seeds[2], (C,), 0.5, 3.0, (), jnp.float32)
    out_weight = noise(seeds[3], (27, C, 3), (27 * C) ** -0.5, 0.125)
    out_bias = noise(seeds[4], (3,), 0.5, 3.0, (), jnp.float32)
    target_frames = draw_target_frames(jax.random.fold_in(seeds[6], 71), 0)
    return dict(latent_features=latent_features, conv_weight=conv_weight, conv_bias=conv_bias, out_weight=out_weight, out_bias=out_bias, target_frames=target_frames)


def tap_conv(padded, weight, frames, rows_out, columns, flipped):
    summed = None
    for kernel_tap in range(27):
        depth_off = kernel_tap // 9
        row_off = kernel_tap // 3 % 3
        col_off = kernel_tap % 3
        if flipped:
            starts = (0, 2 - depth_off, 2 - row_off, 2 - col_off)
            matrix = weight[kernel_tap].T
        else:
            starts = (0, depth_off, row_off, col_off)
            matrix = weight[kernel_tap]
        window = lax.slice(padded, starts, (padded.shape[0], starts[1] + frames, starts[2] + rows_out, starts[3] + columns))
        product = lax.dot_general(matrix.astype(jnp.float32), window.astype(jnp.float32), (((0,), (0,)), ((), ())))
        summed = product if summed is None else summed + product
    return summed

def tap_grads(padded, grad, frames, rows_out, columns):
    results = []
    for kernel_tap in range(27):
        depth_off = kernel_tap // 9
        row_off = kernel_tap // 3 % 3
        col_off = kernel_tap % 3
        window = lax.slice(padded, (0, depth_off, row_off, col_off), (padded.shape[0], depth_off + frames, row_off + rows_out, col_off + columns))
        results.append(lax.dot_general(window.astype(jnp.float32), grad.astype(jnp.float32), (((1, 2, 3), (1, 2, 3)), ((), ()))))
    return jnp.stack(results)

def reference(latent_features, conv_weight, conv_bias, out_weight, out_bias, target_frames):
    loss_scale = 1.0 / math.sqrt(3 * CLIPS * F * H * W)

    def one_clip(inputs):
        latent, target = inputs
        padded_in = jnp.pad(latent, ((0, 0), (2, 0), (1, 1), (1, 1)))
        pre_act = tap_conv(padded_in, conv_weight, F, H, W, False) + conv_bias[:, None, None, None]
        sig_pre = jax.nn.sigmoid(pre_act)
        hidden = (pre_act * sig_pre).astype(jnp.bfloat16)
        padded_hidden = jnp.pad(hidden, ((0, 0), (2, 0), (1, 1), (1, 1)))
        out_pre = tap_conv(padded_hidden, out_weight, F, H, W, False) + out_bias[:, None, None, None]
        decoded = out_pre.astype(jnp.bfloat16)
        grad_frames = ((decoded.astype(jnp.float32) - target.astype(jnp.float32)) * loss_scale).astype(jnp.bfloat16)
        padded_grad = jnp.pad(grad_frames, ((0, 0), (0, 2), (1, 1), (1, 1)))
        backed = tap_conv(padded_grad, out_weight, F, H, W, True)
        grad_hidden = (backed * sig_pre * (1.0 + pre_act * (1.0 - sig_pre))).astype(jnp.bfloat16)
        grad_conv = tap_grads(padded_in, grad_hidden, F, H, W)
        grad_cbias = lax.optimization_barrier(jnp.sum(grad_hidden.astype(jnp.float32), axis=(1, 2, 3)))
        grad_outw = tap_grads(padded_hidden, grad_frames, F, H, W)
        grad_obias = lax.optimization_barrier(jnp.sum(grad_frames.astype(jnp.float32), axis=(1, 2, 3)))
        return (decoded, grad_conv, grad_cbias, grad_outw, grad_obias)
    decoded, grad_conv, grad_cbias, grad_outw, grad_obias = lax.map(one_clip, (latent_features, target_frames))
    return (decoded, lax.optimization_barrier(jnp.sum(grad_conv, axis=0)), lax.optimization_barrier(jnp.sum(grad_cbias, axis=0)), lax.optimization_barrier(jnp.sum(grad_outw, axis=0)), lax.optimization_barrier(jnp.sum(grad_obias, axis=0)))
```

```python
import functools
import math

import jax
import jax.numpy as jnp
from jax import lax
from jax.experimental import pallas as pl
from jax.experimental.pallas import tpu as pltpu
from jax.sharding import Mesh, PartitionSpec as P

BF = jnp.bfloat16
F32 = jnp.float32
C = 96
F = 5
W = 128
TAPS = 27
TPAD = 28
OPAD = 8
GROWS = TPAD * OPAD
HR = 4
FW = HR * W
POS = F * FW
KT = 9 * C
NW = TAPS * C
MAIN = 1920
TAIL = NW - MAIN
ROWS = 2048
EDGE_AXES = ("x", "zl", "y")
PLANE = ("x", "y", "c")
DEPTH = ("zl", "zh")


def nt(a, b):
    return lax.dot_general(a, b, (((1,), (1,)), ((), ())), preferred_element_type=F32)


def nn(a, b):
    return lax.dot_general(a, b, (((1,), (0,)), ((), ())), preferred_element_type=F32)


def tn(a, b):
    return lax.dot_general(a, b, (((0,), (0,)), ((), ())), preferred_element_type=F32)


def shifted(v, lane, by):
    if by == 0:
        return v
    if by > 0:
        return jnp.where(lane < W - 1, pltpu.roll(v, W - 1, 1), 0.0)
    return jnp.where(lane > 0, pltpu.roll(v, 1, 1), 0.0)


def device_kernel(
    n_rows, scale,
    own_ref, pair_ref, wt_ref, cb_ref, wo_ref, ob_ref, tgt_ref,
    dec_ref, pay_ref,
    q_ref, hid_ref, fac_ref, y_ref, g_ref, gh_ref, main_ref,
):
    row_id = (lax.axis_index("x") * lax.axis_size("zl") + lax.axis_index("zl")) * lax.axis_size(
        "y"
    ) + lax.axis_index("y")
    odd = lax.rem(row_id, 2)
    first = row_id == 0
    last = row_id == n_rows - 1
    lane96 = lax.broadcasted_iota(jnp.int32, (C, W), 1)
    lane8 = lax.broadcasted_iota(jnp.int32, (OPAD, W), 1)

    for g in range(F):
        for r in range(6):
            if r < 2:
                tile = pair_ref[1 - odd, g, r]
            elif r < 4:
                tile = own_ref[g, r - 2]
            else:
                tile = pair_ref[odd, g, r - 4]
            wide = tile.astype(F32)
            for kj in range(3):
                piece = tile if kj == 1 else shifted(wide, lane96, kj - 1).astype(BF)
                for ki in range(3):
                    i = r - ki
                    if 0 <= i < HR:
                        base = (ki * 3 + kj) * C
                        q_ref[base : base + C, g * FW + i * W : g * FW + (i + 1) * W] = piece

    srow = lax.broadcasted_iota(jnp.int32, (C, GROWS), 0)
    scol = lax.broadcasted_iota(jnp.int32, (C, GROWS), 1)
    pick = ((srow // 32 == scol % OPAD) & (srow % 32 == scol // OPAD)).astype(F32).astype(BF)
    wo = wo_ref[...]
    wo8 = tn(pick, wo).astype(BF)
    wo8t = tn(wo, pick).astype(BF)

    col = lax.broadcasted_iota(jnp.int32, (1, FW), 1)
    outside = ((col < W) & first) | ((col >= 3 * W) & last)
    keep = jnp.where(outside, 0.0, 1.0)
    for f in range(F):
        pre = None
        for kt in range(3):
            g = f + kt - 2
            if g < 0:
                continue
            part = nn(wt_ref[:, kt * KT : (kt + 1) * KT], q_ref[:, g * FW : (g + 1) * FW])
            pre = part if pre is None else pre + part
        pre = pre + cb_ref[...]
        sig = jax.nn.sigmoid(pre)
        hid = (pre * sig * keep).astype(BF)
        hid_ref[:, f * FW : (f + 1) * FW] = hid
        fac_ref[:, f * FW : (f + 1) * FW] = sig * (1.0 + pre * (1.0 - sig)) * keep
        y_ref[:, f * FW : (f + 1) * FW] = nn(wo8, hid)

    grads = {}
    obsum = jnp.zeros((OPAD, W), F32)
    for f in range(F):
        for i in range(2):
            dec = None
            for kj in range(3):
                z = None
                for kt in range(3):
                    g = f + kt - 2
                    if g < 0:
                        continue
                    for ki in range(3):
                        t = kt * 9 + ki * 3 + kj
                        at = g * FW + (i + ki) * W
                        v = y_ref[t * OPAD : (t + 1) * OPAD, at : at + W]
                        z = v if z is None else z + v
                z = shifted(z, lane8, kj - 1)
                dec = z if dec is None else dec + z
            dec = (dec + ob_ref[...]).astype(BF)
            at = (f * 2 + i) * W
            dec_ref[:, at : at + W] = dec.astype(F32)
            gf = ((dec.astype(F32) - tgt_ref[:, at : at + W]) * scale).astype(BF).astype(F32)
            obsum = obsum + gf
            for kj in range(3):
                grads[f, i, kj] = shifted(gf, lane8, 1 - kj)

    none = jnp.zeros((OPAD, W), F32)
    for g in range(F):
        for i in range(HR):
            parts = []
            for t in range(TPAD):
                kt, ki, kj = t // 9, t // 3 % 3, t % 3
                parts.append(grads.get((g + 2 - kt, i - ki, kj), none) if t < TAPS else none)
            at = g * FW + i * W
            for p in range(TPAD // 2):
                both = jnp.concatenate(parts[2 * p : 2 * p + 2], axis=0).astype(BF)
                g_ref[p * 16 : (p + 1) * 16, at : at + W] = both

    gh_ref[C:, :] = jnp.zeros((W - C, POS), BF)
    for f in range(F):
        back = nn(wo8t, g_ref[:, f * FW : (f + 1) * FW])
        gh_ref[:C, f * FW : (f + 1) * FW] = (back * fac_ref[:, f * FW : (f + 1) * FW]).astype(BF)

    for kt in range(3):
        main_ref[kt * KT : (kt + 1) * KT, :] = nt(
            q_ref[:, : (3 + kt) * FW], gh_ref[:, (2 - kt) * FW :]
        )
    gow = nt(g_ref[...], hid_ref[...]).astype(BF)
    gow = nn(pick, gow)
    bias = nt(jnp.ones((OPAD, POS), BF), gh_ref[...])
    obias = jnp.broadcast_to(jnp.sum(obsum, axis=1, keepdims=True), (OPAD, W))

    for k in range(3):
        lo, hi = k * TAIL, (k + 1) * TAIL
        tail = pltpu.roll(main_ref[MAIN:, :], 96 - 32 * k, 1)
        if hi <= MAIN:
            head = main_ref[lo:hi, :]
        else:
            head = jnp.concatenate(
                [main_ref[lo:MAIN, :], jnp.pad(gow, ((0, 0), (0, W - C)))], axis=0
            )
        lane = lax.broadcasted_iota(jnp.int32, (TAIL, W), 1)
        pay_ref[lo:hi, :] = jnp.where(lane < C, head, tail).astype(BF)
    for at, v in ((2016, bias), (2032, obias)):
        top = v.astype(BF).astype(F32)
        pay_ref[at : at + 16, :] = jnp.concatenate([top, v - top], axis=0).astype(BF)


def split_sums(total, is_last):
    out = total.astype(BF)
    fixed = []
    for at in (32, 48):
        whole = total[at : at + 8] + total[at + 8 : at + 16]
        top = whole.astype(BF).astype(F32)
        fixed += [top, whole - top]
    special = jnp.concatenate([total[:32]] + fixed, axis=0).astype(BF)
    return jnp.where(is_last, special, out)


def sum_kernel(copies, in_ref, out_ref):
    total = in_ref[0].astype(F32)
    for k in range(1, in_ref.shape[0]):
        total = total + in_ref[k].astype(F32)
    index = (lax.axis_index("x") * lax.axis_size("y") + lax.axis_index("y")) * lax.axis_size(
        "c"
    ) + lax.axis_index("c")
    count = lax.axis_size("x") * lax.axis_size("y") * lax.axis_size("c")
    res = split_sums(total, index == count - 1)
    for k in range(copies):
        out_ref[k] = res


def unpack_kernel(in_ref, gw_ref, gb_ref, go_ref, gob_ref):
    gw_ref[:MAIN, :] = in_ref[:MAIN, :C].astype(F32)
    lane = lax.broadcasted_iota(jnp.int32, (TAIL, W), 1)
    tail = None
    for k in range(3):
        v = pltpu.roll(in_ref[k * TAIL : (k + 1) * TAIL, :].astype(F32), 32 + 32 * k, 1)
        tail = v if tail is None else jnp.where(lane < 32 * k, tail, v)
    gw_ref[MAIN:, :] = tail[:, :C]
    gow = in_ref[MAIN : MAIN + 96, :].astype(F32)
    for o in range(3):
        go_ref[o] = gow[o * 32 : o * 32 + TAPS, :C]
    sums = in_ref[2016:2048, :].astype(F32)
    gb_ref[...] = (sums[0:8] + sums[8:16])[0:1, :C]
    ob = sums[16:24] + sums[24:32]
    r8 = lax.broadcasted_iota(jnp.int32, (OPAD, W), 0)
    l8 = lax.broadcasted_iota(jnp.int32, (OPAD, W), 1)
    gob_ref[...] = jnp.sum(jnp.where(r8 == l8, ob, 0.0), axis=0, keepdims=True)


VM = functools.partial(pl.BlockSpec, memory_space=pltpu.VMEM)
LIMIT = 48 * 1024 * 1024


def local(latent_features, conv_weight, conv_bias, out_weight, out_bias, target_frames):
    sizes = [lax.axis_size(a) for a in EDGE_AXES]
    n_rows = sizes[0] * sizes[1] * sizes[2]
    clips = lax.axis_size("zh") * lax.axis_size("c")
    scale = 1.0 / math.sqrt(3 * clips * F * 2 * n_rows * W)

    own = jnp.transpose(latent_features[0], (1, 2, 0, 3))
    near = [(i, i ^ 1) for i in range(n_rows)]
    far = [(i, ((i + 1) ^ 1) - 1) for i in range(1, n_rows - 1)]
    pair = jnp.stack([lax.ppermute(own, EDGE_AXES, near), lax.ppermute(own, EDGE_AXES, far)])

    wt = jnp.transpose(conv_weight, (2, 0, 1)).reshape(C, NW)
    wo = jnp.pad(jnp.transpose(out_weight, (2, 0, 1)), ((0, 0), (0, 5), (0, 0))).reshape(C, C)
    ob = jnp.pad(out_bias[:, None], ((0, 5), (0, 0)))
    tgt = jnp.pad(target_frames[0].reshape(3, F * 2 * W).astype(F32), ((0, 5), (0, 0)))

    dec, packed = pl.pallas_call(
        functools.partial(device_kernel, n_rows, scale),
        out_shape=(
            jax.ShapeDtypeStruct((OPAD, F * 2 * W), F32),
            jax.ShapeDtypeStruct((ROWS, W), BF),
        ),
        in_specs=[VM()] * 7,
        out_specs=(VM(), VM()),
        scratch_shapes=[
            pltpu.VMEM((KT, POS), BF),
            pltpu.VMEM((C, POS), BF),
            pltpu.VMEM((C, POS), F32),
            pltpu.VMEM((GROWS, POS), F32),
            pltpu.VMEM((GROWS, POS), BF),
            pltpu.VMEM((W, POS), BF),
            pltpu.VMEM((NW, W), F32),
        ],
        compiler_params=pltpu.CompilerParams(vmem_limit_bytes=LIMIT),
        name="device_part",
    )(own, pair, wt, conv_bias[:, None], wo, ob, tgt)

    plane = lax.axis_size("x") * lax.axis_size("y") * lax.axis_size("c")
    depth = lax.axis_size("zl") * lax.axis_size("zh")
    chunk = ROWS // plane

    def summed(parts, copies):
        return pl.pallas_call(
            functools.partial(sum_kernel, copies),
            out_shape=jax.ShapeDtypeStruct((copies, chunk, W), BF),
            in_specs=[VM()],
            out_specs=VM(),
            name="sum_parts",
        )(parts)

    parts = lax.all_to_all(packed.reshape(plane, chunk, W), PLANE, 0, 0)
    parts = lax.all_to_all(summed(parts, depth), DEPTH, 0, 0)
    parts = lax.all_to_all(summed(parts, plane), PLANE, 0, 0)

    gw, gb, go, gob = pl.pallas_call(
        unpack_kernel,
        out_shape=(
            jax.ShapeDtypeStruct((NW, C), F32),
            jax.ShapeDtypeStruct((1, C), F32),
            jax.ShapeDtypeStruct((3, TAPS, C), F32),
            jax.ShapeDtypeStruct((1, W), F32),
        ),
        in_specs=[VM()],
        out_specs=(VM(),) * 4,
        name="unpack",
    )(parts.reshape(ROWS, W))
    decoded = dec[:3].astype(BF).reshape(1, 3, F, 2, W)
    return (
        decoded,
        gw.reshape(TAPS, C, C),
        gb.reshape(C),
        jnp.transpose(go, (1, 2, 0)),
        gob[0, :3],
    )


def solution(mesh):
    split = Mesh(mesh.devices.reshape(4, 4, 4, 4, 2), ("x", "zl", "y", "zh", "c"))
    frames = P(("zh", "c"), None, None, EDGE_AXES, None)
    return jax.shard_map(
        local,
        mesh=split,
        in_specs=(frames, P(), P(), P(), P(), frames),
        out_specs=(frames, P(), P(), P(), P()),
        check_vma=False,
    )
```

```python
import functools
import math

import jax
import jax.numpy as jnp
from jax import lax
from jax.experimental import pallas as pl
from jax.experimental.pallas import tpu as pltpu
from jax.sharding import Mesh, PartitionSpec as P

BF = jnp.bfloat16
F32 = jnp.float32
C = 96
F = 5
W = 128
TAPS = 27
TPAD = 28
OPAD = 8
GROWS = TPAD * OPAD
HR = 4
FW = HR * W
POS = F * FW
KT = 9 * C
NW = TAPS * C
MAIN = 1920
TAIL = NW - MAIN
ROWS = 2048
EDGE_AXES = ("x", "z1", "z0", "y")
NEAR = ("x", "z0", "y", "c")
DEPTH = ("z1", "zh")


def nt(a, b):
    return lax.dot_general(a, b, (((1,), (1,)), ((), ())), preferred_element_type=F32)


def nn(a, b):
    return lax.dot_general(a, b, (((1,), (0,)), ((), ())), preferred_element_type=F32)


def tn(a, b):
    return lax.dot_general(a, b, (((0,), (0,)), ((), ())), preferred_element_type=F32)


def shifted(v, lane, by):
    if by == 0:
        return v
    if by > 0:
        return jnp.where(lane < W - 1, pltpu.roll(v, W - 1, 1), 0.0)
    return jnp.where(lane > 0, pltpu.roll(v, 1, 1), 0.0)


def flat_index(axes):
    index = 0
    for axis in axes:
        index = index * lax.axis_size(axis) + lax.axis_index(axis)
    return index


def device_kernel(
    n_rows, scale,
    own_ref, pair_ref, wt_ref, cb_ref, wo_ref, ob_ref, tgt_ref,
    dec_ref, pay_ref,
    q_ref, r_ref, hid_ref, fac_ref, y_ref, g_ref, gh_ref, main_ref,
):
    row_id = flat_index(EDGE_AXES)
    odd = lax.rem(row_id, 2)
    first = row_id == 0
    last = row_id == n_rows - 1
    lane96 = lax.broadcasted_iota(jnp.int32, (C, W), 1)
    lane8 = lax.broadcasted_iota(jnp.int32, (OPAD, W), 1)

    for g in range(F):
        for r in range(6):
            if r < 2:
                tile = pair_ref[1 - odd, g, r]
            elif r < 4:
                tile = own_ref[g, r - 2]
            else:
                tile = pair_ref[odd, g, r - 4]
            wide = tile.astype(F32)
            for kj in range(3):
                piece = tile if kj == 1 else shifted(wide, lane96, kj - 1).astype(BF)
                for ki in range(3):
                    i = r - ki
                    if 0 <= i < HR:
                        base = (ki * 3 + kj) * C
                        q_ref[base : base + C, g * FW + i * W : g * FW + (i + 1) * W] = piece

    srow = lax.broadcasted_iota(jnp.int32, (C, GROWS), 0)
    scol = lax.broadcasted_iota(jnp.int32, (C, GROWS), 1)
    pick = ((srow // 32 == scol % OPAD) & (srow % 32 == scol // OPAD)).astype(F32).astype(BF)
    wo = wo_ref[...]
    wo8 = tn(pick, wo).astype(BF)
    wo8t = tn(wo, pick).astype(BF)

    col = lax.broadcasted_iota(jnp.int32, (1, FW), 1)
    outside = ((col < W) & first) | ((col >= 3 * W) & last)
    keep = jnp.where(outside, 0.0, 1.0)
    for f in range(F):
        low = max(0, f - 2) * C
        r_ref[f, low:, :] = nn(wt_ref[low:, :], q_ref[:, f * FW : (f + 1) * FW])
        pre = cb_ref[...]
        for kt in range(2, max(-1, 1 - f), -1):
            pre = pre + r_ref[f + kt - 2, kt * C : (kt + 1) * C, :]
        sig = jax.nn.sigmoid(pre)
        hid = (pre * sig * keep).astype(BF)
        hid_ref[:, f * FW : (f + 1) * FW] = hid
        fac_ref[:, f * FW : (f + 1) * FW] = sig * (1.0 + pre * (1.0 - sig)) * keep
        y_ref[:, f * FW : (f + 1) * FW] = nn(wo8, hid)

    grads = {}
    obsum = jnp.zeros((OPAD, W), F32)
    for f in range(F):
        decs = []
        for i in range(2):
            dec = None
            for kj in range(3):
                z = None
                for kt in range(3):
                    g = f + kt - 2
                    if g < 0:
                        continue
                    for ki in range(3):
                        t = kt * 9 + ki * 3 + kj
                        at = g * FW + (i + ki) * W
                        v = y_ref[t * OPAD : (t + 1) * OPAD, at : at + W]
                        z = v if z is None else z + v
                z = shifted(z, lane8, kj - 1)
                dec = z if dec is None else dec + z
            dec = (dec + ob_ref[...]).astype(BF)
            at = (f * 2 + i) * W
            decs.append(dec.astype(F32))
            gf = ((dec.astype(F32) - tgt_ref[:, at : at + W]) * scale).astype(BF).astype(F32)
            obsum = obsum + gf
            for kj in range(3):
                grads[f, i, kj] = shifted(gf, lane8, 1 - kj)
        for o in range(3):
            rows = jnp.concatenate([d[o : o + 1] for d in decs], axis=0)
            dec_ref[0, o, f] = rows.astype(BF)

    none = jnp.zeros((OPAD, W), F32)
    for g in range(F):
        for i in range(HR):
            parts = []
            for t in range(TPAD):
                kt, ki, kj = t // 9, t // 3 % 3, t % 3
                parts.append(grads.get((g + 2 - kt, i - ki, kj), none) if t < TAPS else none)
            at = g * FW + i * W
            for p in range(TPAD // 2):
                both = jnp.concatenate(parts[2 * p : 2 * p + 2], axis=0).astype(BF)
                g_ref[p * 16 : (p + 1) * 16, at : at + W] = both

    gh_ref[C:W, :] = jnp.zeros((W - C, POS), BF)
    gh_ref[W + C :, :] = jnp.zeros((W - C, POS), BF)
    gh_ref[W:, POS - FW :] = jnp.zeros((W, FW), BF)
    for f in range(F):
        back = nn(wo8t, g_ref[:, f * FW : (f + 1) * FW])
        gh = (back * fac_ref[:, f * FW : (f + 1) * FW]).astype(BF)
        gh_ref[:C, f * FW : (f + 1) * FW] = gh
        if f:
            gh_ref[W : W + C, (f - 1) * FW : f * FW] = gh

    both = nt(q_ref[...], gh_ref[...])
    main_ref[2 * KT :, :] = both[:, :W]
    main_ref[KT : 2 * KT, :] = both[:, W:]
    main_ref[:KT, :] = nt(q_ref[:, : 3 * FW], gh_ref[:W, 2 * FW :])
    gow = nt(g_ref[...], hid_ref[...]).astype(BF)
    gow = nn(pick, gow)
    bias = nt(jnp.ones((OPAD, POS), BF), gh_ref[:W, :])
    obias = jnp.broadcast_to(jnp.sum(obsum, axis=1, keepdims=True), (OPAD, W))

    lane = lax.broadcasted_iota(jnp.int32, (TAIL, W), 1)
    for k in range(3):
        lo, hi = k * TAIL, (k + 1) * TAIL
        tail = pltpu.roll(main_ref[MAIN:, :], 96 - 32 * k, 1)
        if hi <= MAIN:
            head = main_ref[lo:hi, :]
        else:
            head = jnp.concatenate(
                [main_ref[lo:MAIN, :], jnp.pad(gow, ((0, 0), (0, W - C)))], axis=0
            )
        pay_ref[lo:hi, :] = jnp.where(lane < C, head, tail).astype(BF)
    for at, v in ((2016, bias), (2032, obias)):
        top = v.astype(BF).astype(F32)
        pay_ref[at : at + 16, :] = jnp.concatenate([top, v - top], axis=0).astype(BF)


def split_sums(total, is_last):
    out = total.astype(BF)
    start = total.shape[0] - 32
    fixed = []
    for at in (start, start + 16):
        whole = total[at : at + 8] + total[at + 8 : at + 16]
        top = whole.astype(BF).astype(F32)
        fixed += [top, whole - top]
    special = jnp.concatenate(([total[:start]] if start else []) + fixed, axis=0).astype(BF)
    return jnp.where(is_last, special, out)


def sum_kernel(in_ref, out_ref):
    total = in_ref[0].astype(F32)
    for k in range(1, in_ref.shape[0]):
        total = total + in_ref[k].astype(F32)
    count = math.prod(lax.axis_size(a) for a in NEAR)
    res = split_sums(total, flat_index(NEAR) == count - 1)
    for k in range(out_ref.shape[0]):
        out_ref[k] = res


def unpack_kernel(in_ref, gw_ref, gb_ref, go_ref, gob_ref):
    def get(lo, hi):
        return in_ref[lo:hi, :].astype(F32)

    gw_ref[:MAIN, :] = get(0, MAIN)[:, :C]
    lane = lax.broadcasted_iota(jnp.int32, (TAIL, W), 1)
    tail = None
    for k in range(3):
        v = pltpu.roll(get(k * TAIL, (k + 1) * TAIL), 32 + 32 * k, 1)
        tail = v if tail is None else jnp.where(lane < 32 * k, tail, v)
    gw_ref[MAIN:, :] = tail[:, :C]
    gow = get(MAIN, MAIN + 96)
    for o in range(3):
        go_ref[o] = gow[o * 32 : o * 32 + TAPS, :C]
    sums = get(2016, 2048)
    gb_ref[...] = (sums[0:8] + sums[8:16])[0, :C]
    ob = sums[16:24] + sums[24:32]
    r8 = lax.broadcasted_iota(jnp.int32, (OPAD, W), 0)
    l8 = lax.broadcasted_iota(jnp.int32, (OPAD, W), 1)
    gob_ref[...] = jnp.sum(jnp.where(r8 == l8, ob, 0.0), axis=0)[:3]


VM = functools.partial(pl.BlockSpec, memory_space=pltpu.VMEM)
LIMIT = 48 * 1024 * 1024
SMALL = 4 * 1024 * 1024


def k1_call(n_rows, scale):
    return pl.pallas_call(
        functools.partial(device_kernel, n_rows, scale),
        out_shape=(
            jax.ShapeDtypeStruct((1, 3, F, 2, W), BF),
            jax.ShapeDtypeStruct((ROWS, W), BF),
        ),
        in_specs=[VM()] * 7,
        out_specs=(VM(), VM()),
        scratch_shapes=[
            pltpu.VMEM((KT, POS), BF),
            pltpu.VMEM((F, 3 * C, FW), F32),
            pltpu.VMEM((C, POS), BF),
            pltpu.VMEM((C, POS), F32),
            pltpu.VMEM((GROWS, POS), F32),
            pltpu.VMEM((GROWS, POS), BF),
            pltpu.VMEM((2 * W, POS), BF),
            pltpu.VMEM((NW, W), F32),
        ],
        compiler_params=pltpu.CompilerParams(vmem_limit_bytes=LIMIT),
        name="device_part",
    )


def local(latent_features, conv_weight, conv_bias, out_weight, out_bias, target_frames):
    sizes = [lax.axis_size(a) for a in EDGE_AXES]
    n_rows = math.prod(sizes)
    clips = lax.axis_size("zh") * lax.axis_size("c")
    scale = 1.0 / math.sqrt(3 * clips * F * 2 * n_rows * W)

    own = jnp.transpose(latent_features[0], (1, 2, 0, 3))
    even = [(i, i ^ 1) for i in range(n_rows)]
    odd = [(i, ((i + 1) ^ 1) - 1) for i in range(1, n_rows - 1)]
    pair = jnp.stack([lax.ppermute(own, EDGE_AXES, even), lax.ppermute(own, EDGE_AXES, odd)])

    wt = jnp.transpose(conv_weight.reshape(3, KT, C), (0, 2, 1)).reshape(3 * C, KT)
    wo = jnp.pad(jnp.transpose(out_weight, (2, 0, 1)), ((0, 0), (0, 5), (0, 0))).reshape(C, C)
    ob = jnp.pad(out_bias[:, None], ((0, 5), (0, 0)))
    tgt = jnp.pad(target_frames[0].reshape(3, F * 2 * W).astype(F32), ((0, 5), (0, 0)))

    decoded, packed = k1_call(n_rows, scale)(own, pair, wt, conv_bias[:, None], wo, ob, tgt)

    near = math.prod(lax.axis_size(a) for a in NEAR)
    depth = math.prod(lax.axis_size(a) for a in DEPTH)
    chunk = ROWS // near

    def summed(parts, copies):
        return pl.pallas_call(
            sum_kernel,
            out_shape=jax.ShapeDtypeStruct((copies, chunk, W), BF),
            in_specs=[VM()],
            out_specs=VM(),
            compiler_params=pltpu.CompilerParams(vmem_limit_bytes=SMALL),
            name="sum_parts",
        )(parts)

    parts = lax.all_to_all(packed.reshape(near, chunk, W), NEAR, 0, 0)
    parts = lax.all_to_all(summed(parts, depth), DEPTH, 0, 0)
    parts = lax.all_to_all(summed(parts, near), NEAR, 0, 0)

    gw, gb, go, gob = pl.pallas_call(
        unpack_kernel,
        out_shape=(
            jax.ShapeDtypeStruct((NW, C), F32),
            jax.ShapeDtypeStruct((C,), F32),
            jax.ShapeDtypeStruct((3, TAPS, C), F32),
            jax.ShapeDtypeStruct((3,), F32),
        ),
        in_specs=[VM()],
        out_specs=(VM(),) * 4,
        compiler_params=pltpu.CompilerParams(vmem_limit_bytes=2 * SMALL),
        name="unpack",
    )(parts.reshape(ROWS, W))
    return (
        decoded,
        gw.reshape(TAPS, C, C),
        gb,
        jnp.transpose(go, (1, 2, 0)),
        gob,
    )


def solution(mesh):
    split = Mesh(mesh.devices.reshape(4, 2, 2, 4, 4, 2), ("x", "z1", "z0", "y", "zh", "c"))
    frames = P(("zh", "c"), None, None, EDGE_AXES, None)
    return jax.shard_map(
        local,
        mesh=split,
        in_specs=(frames, P(), P(), P(), P(), frames),
        out_specs=(frames, P(), P(), P(), P()),
        check_vma=False,
    )
```

```python
import functools
import math

import jax
import jax.numpy as jnp
from jax import lax
from jax.experimental import pallas as pl
from jax.experimental.pallas import tpu as pltpu
from jax.sharding import Mesh, PartitionSpec as P

BF = jnp.bfloat16
F32 = jnp.float32
C = 96
F = 5
W = 128
TAPS = 27
TPAD = 28
OPAD = 8
GROWS = TPAD * OPAD
HR = 4
FW = HR * W
POS = F * FW
KT = 9 * C
NW = TAPS * C
MAIN = 1920
TAIL = NW - MAIN
ROWS = 2048
EDGE_AXES = ("x", "z1", "z0", "y")
NEAR = ("x", "z0", "y", "c")
DEPTH = ("z1", "zh")


def nt(a, b):
    return lax.dot_general(a, b, (((1,), (1,)), ((), ())), preferred_element_type=F32)


def nn(a, b):
    return lax.dot_general(a, b, (((1,), (0,)), ((), ())), preferred_element_type=F32)


def tn(a, b):
    return lax.dot_general(a, b, (((0,), (0,)), ((), ())), preferred_element_type=F32)


def shifted(v, lane, by):
    if by == 0:
        return v
    if by > 0:
        return jnp.where(lane < W - 1, pltpu.roll(v, W - 1, 1), 0.0)
    return jnp.where(lane > 0, pltpu.roll(v, 1, 1), 0.0)


def flat_index(axes):
    index = 0
    for axis in axes:
        index = index * lax.axis_size(axis) + lax.axis_index(axis)
    return index


def device_kernel(
    n_rows, scale,
    own_ref, pair_ref, wt_ref, cb_ref, wo_ref, ob_ref, tgt_ref,
    dec_ref, pay_ref,
    q_ref, r_ref, hid_ref, fac_ref, y_ref, g_ref, gh_ref, main_ref,
):
    row_id = flat_index(EDGE_AXES)
    odd = lax.rem(row_id, 2)
    first = row_id == 0
    last = row_id == n_rows - 1
    lane96 = lax.broadcasted_iota(jnp.int32, (C, W), 1)
    lane8 = lax.broadcasted_iota(jnp.int32, (OPAD, W), 1)

    for g in range(F):
        for r in range(6):
            if r < 2:
                tile = pair_ref[1 - odd, g, r]
            elif r < 4:
                tile = own_ref[g, r - 2]
            else:
                tile = pair_ref[odd, g, r - 4]
            wide = tile.astype(F32)
            for kj in range(3):
                piece = tile if kj == 1 else shifted(wide, lane96, kj - 1).astype(BF)
                for ki in range(3):
                    i = r - ki
                    if 0 <= i < HR:
                        base = (ki * 3 + kj) * C
                        q_ref[base : base + C, g * FW + i * W : g * FW + (i + 1) * W] = piece

    srow = lax.broadcasted_iota(jnp.int32, (C, GROWS), 0)
    scol = lax.broadcasted_iota(jnp.int32, (C, GROWS), 1)
    pick = ((srow // 32 == scol % OPAD) & (srow % 32 == scol // OPAD)).astype(F32).astype(BF)
    wo = wo_ref[...]
    wo8 = tn(pick, wo).astype(BF)
    wo8t = tn(wo, pick).astype(BF)

    col = lax.broadcasted_iota(jnp.int32, (1, FW), 1)
    outside = ((col < W) & first) | ((col >= 3 * W) & last)
    keep = jnp.where(outside, 0.0, 1.0)
    def conv(f):
        low = max(0, f - 2) * C
        r_ref[f, low:, :] = nn(wt_ref[low:, :], q_ref[:, f * FW : (f + 1) * FW])

    def activate(f):
        pre = cb_ref[...]
        for kt in range(2, max(-1, 1 - f), -1):
            pre = pre + r_ref[f + kt - 2, kt * C : (kt + 1) * C, :]
        sig = jax.nn.sigmoid(pre)
        hid_ref[:, f * FW : (f + 1) * FW] = (pre * sig * keep).astype(BF)
        fac_ref[:, f * FW : (f + 1) * FW] = sig * (1.0 + pre * (1.0 - sig)) * keep

    def project(f):
        y_ref[:, f * FW : (f + 1) * FW] = nn(wo8, hid_ref[:, f * FW : (f + 1) * FW])

    for f in range(F + 2):
        if f < F:
            conv(f)
        if 1 <= f <= F:
            activate(f - 1)
        if f >= 2:
            project(f - 2)

    grads = {}
    obsum = jnp.zeros((OPAD, W), F32)
    for f in range(F):
        decs = []
        for i in range(2):
            dec = None
            for kj in range(3):
                z = None
                for kt in range(3):
                    g = f + kt - 2
                    if g < 0:
                        continue
                    for ki in range(3):
                        t = kt * 9 + ki * 3 + kj
                        at = g * FW + (i + ki) * W
                        v = y_ref[t * OPAD : (t + 1) * OPAD, at : at + W]
                        z = v if z is None else z + v
                z = shifted(z, lane8, kj - 1)
                dec = z if dec is None else dec + z
            dec = (dec + ob_ref[...]).astype(BF)
            at = (f * 2 + i) * W
            decs.append(dec.astype(F32))
            gf = ((dec.astype(F32) - tgt_ref[:, at : at + W]) * scale).astype(BF).astype(F32)
            obsum = obsum + gf
            for kj in range(3):
                grads[f, i, kj] = shifted(gf, lane8, 1 - kj)
        for o in range(3):
            rows = jnp.concatenate([d[o : o + 1] for d in decs], axis=0)
            dec_ref[0, o, f] = rows.astype(BF)

    none = jnp.zeros((OPAD, W), F32)
    for g in range(F):
        for i in range(HR):
            parts = []
            for t in range(TPAD):
                kt, ki, kj = t // 9, t // 3 % 3, t % 3
                parts.append(grads.get((g + 2 - kt, i - ki, kj), none) if t < TAPS else none)
            at = g * FW + i * W
            for p in range(TPAD // 2):
                both = jnp.concatenate(parts[2 * p : 2 * p + 2], axis=0).astype(BF)
                g_ref[p * 16 : (p + 1) * 16, at : at + W] = both

    gh_ref[C:W, :] = jnp.zeros((W - C, POS), BF)
    gh_ref[W + C :, :] = jnp.zeros((W - C, POS), BF)
    gh_ref[W:, POS - FW :] = jnp.zeros((W, FW), BF)
    for f in range(F):
        back = nn(wo8t, g_ref[:, f * FW : (f + 1) * FW])
        gh = (back * fac_ref[:, f * FW : (f + 1) * FW]).astype(BF)
        gh_ref[:C, f * FW : (f + 1) * FW] = gh
        if f:
            gh_ref[W : W + C, (f - 1) * FW : f * FW] = gh

    both = nt(q_ref[...], gh_ref[...])
    main_ref[2 * KT :, :] = both[:, :W]
    main_ref[KT : 2 * KT, :] = both[:, W:]
    main_ref[:KT, :] = nt(q_ref[:, : 3 * FW], gh_ref[:W, 2 * FW :])
    gow = nt(g_ref[...], hid_ref[...]).astype(BF)
    gow = nn(pick, gow)
    bias = nt(jnp.ones((OPAD, POS), BF), gh_ref[:W, :])
    obias = jnp.broadcast_to(jnp.sum(obsum, axis=1, keepdims=True), (OPAD, W))

    lane = lax.broadcasted_iota(jnp.int32, (TAIL, W), 1)
    for k in range(3):
        lo, hi = k * TAIL, (k + 1) * TAIL
        tail = pltpu.roll(main_ref[MAIN:, :], 96 - 32 * k, 1)
        if hi <= MAIN:
            head = main_ref[lo:hi, :]
        else:
            head = jnp.concatenate(
                [main_ref[lo:MAIN, :], jnp.pad(gow, ((0, 0), (0, W - C)))], axis=0
            )
        pay_ref[lo:hi, :] = jnp.where(lane < C, head, tail).astype(BF)
    for at, v in ((2016, bias), (2032, obias)):
        top = v.astype(BF).astype(F32)
        pay_ref[at : at + 16, :] = jnp.concatenate([top, v - top], axis=0).astype(BF)


def split_sums(total, is_last):
    out = total.astype(BF)
    start = total.shape[0] - 32
    fixed = []
    for at in (start, start + 16):
        whole = total[at : at + 8] + total[at + 8 : at + 16]
        top = whole.astype(BF).astype(F32)
        fixed += [top, whole - top]
    special = jnp.concatenate(([total[:start]] if start else []) + fixed, axis=0).astype(BF)
    return jnp.where(is_last, special, out)


def sum_kernel(in_ref, out_ref):
    total = in_ref[0].astype(F32)
    for k in range(1, in_ref.shape[0]):
        total = total + in_ref[k].astype(F32)
    count = math.prod(lax.axis_size(a) for a in NEAR)
    res = split_sums(total, flat_index(NEAR) == count - 1)
    for k in range(out_ref.shape[0]):
        out_ref[k] = res


def unpack_kernel(in_ref, gw_ref, gb_ref, go_ref, gob_ref):
    def get(lo, hi):
        return in_ref[lo:hi, :].astype(F32)

    gw_ref[:MAIN, :] = get(0, MAIN)[:, :C]
    lane = lax.broadcasted_iota(jnp.int32, (TAIL, W), 1)
    tail = None
    for k in range(3):
        v = pltpu.roll(get(k * TAIL, (k + 1) * TAIL), 32 + 32 * k, 1)
        tail = v if tail is None else jnp.where(lane < 32 * k, tail, v)
    gw_ref[MAIN:, :] = tail[:, :C]
    gow = get(MAIN, MAIN + 96)
    for o in range(3):
        go_ref[o] = gow[o * 32 : o * 32 + TAPS, :C]
    sums = get(2016, 2048)
    gb_ref[...] = (sums[0:8] + sums[8:16])[0, :C]
    ob = sums[16:24] + sums[24:32]
    r8 = lax.broadcasted_iota(jnp.int32, (OPAD, W), 0)
    l8 = lax.broadcasted_iota(jnp.int32, (OPAD, W), 1)
    gob_ref[...] = jnp.sum(jnp.where(r8 == l8, ob, 0.0), axis=0)[:3]


VM = functools.partial(pl.BlockSpec, memory_space=pltpu.VMEM)
LIMIT = 48 * 1024 * 1024
SMALL = 4 * 1024 * 1024


def k1_call(n_rows, scale):
    return pl.pallas_call(
        functools.partial(device_kernel, n_rows, scale),
        out_shape=(
            jax.ShapeDtypeStruct((1, 3, F, 2, W), BF),
            jax.ShapeDtypeStruct((ROWS, W), BF),
        ),
        in_specs=[VM()] * 7,
        out_specs=(VM(), VM()),
        scratch_shapes=[
            pltpu.VMEM((KT, POS), BF),
            pltpu.VMEM((F, 3 * C, FW), F32),
            pltpu.VMEM((C, POS), BF),
            pltpu.VMEM((C, POS), F32),
            pltpu.VMEM((GROWS, POS), F32),
            pltpu.VMEM((GROWS, POS), BF),
            pltpu.VMEM((2 * W, POS), BF),
            pltpu.VMEM((NW, W), F32),
        ],
        compiler_params=pltpu.CompilerParams(vmem_limit_bytes=LIMIT),
        name="device_part",
    )


def local(latent_features, conv_weight, conv_bias, out_weight, out_bias, target_frames):
    sizes = [lax.axis_size(a) for a in EDGE_AXES]
    n_rows = math.prod(sizes)
    clips = lax.axis_size("zh") * lax.axis_size("c")
    scale = 1.0 / math.sqrt(3 * clips * F * 2 * n_rows * W)

    own = jnp.transpose(latent_features[0], (1, 2, 0, 3))
    even = [(i, i ^ 1) for i in range(n_rows)]
    odd = [(i, ((i + 1) ^ 1) - 1) for i in range(1, n_rows - 1)]
    pair = jnp.stack([lax.ppermute(own, EDGE_AXES, even), lax.ppermute(own, EDGE_AXES, odd)])

    wt = jnp.transpose(conv_weight.reshape(3, KT, C), (0, 2, 1)).reshape(3 * C, KT)
    wo = jnp.pad(jnp.transpose(out_weight, (2, 0, 1)), ((0, 0), (0, 5), (0, 0))).reshape(C, C)
    ob = jnp.pad(out_bias[:, None], ((0, 5), (0, 0)))
    tgt = jnp.pad(target_frames[0].reshape(3, F * 2 * W).astype(F32), ((0, 5), (0, 0)))

    decoded, packed = k1_call(n_rows, scale)(own, pair, wt, conv_bias[:, None], wo, ob, tgt)

    near = math.prod(lax.axis_size(a) for a in NEAR)
    depth = math.prod(lax.axis_size(a) for a in DEPTH)
    chunk = ROWS // near

    def summed(parts, copies):
        return pl.pallas_call(
            sum_kernel,
            out_shape=jax.ShapeDtypeStruct((copies, chunk, W), BF),
            in_specs=[VM()],
            out_specs=VM(),
            compiler_params=pltpu.CompilerParams(vmem_limit_bytes=SMALL),
            name="sum_parts",
        )(parts)

    parts = lax.all_to_all(packed.reshape(near, chunk, W), NEAR, 0, 0)
    parts = lax.all_to_all(summed(parts, depth), DEPTH, 0, 0)
    parts = lax.all_to_all(summed(parts, near), NEAR, 0, 0)

    gw, gb, go, gob = pl.pallas_call(
        unpack_kernel,
        out_shape=(
            jax.ShapeDtypeStruct((NW, C), F32),
            jax.ShapeDtypeStruct((C,), F32),
            jax.ShapeDtypeStruct((3, TAPS, C), F32),
            jax.ShapeDtypeStruct((3,), F32),
        ),
        in_specs=[VM()],
        out_specs=(VM(),) * 4,
        compiler_params=pltpu.CompilerParams(vmem_limit_bytes=2 * SMALL),
        name="unpack",
    )(parts.reshape(ROWS, W))
    return (
        decoded,
        gw.reshape(TAPS, C, C),
        gb,
        jnp.transpose(go, (1, 2, 0)),
        gob,
    )


def solution(mesh):
    split = Mesh(mesh.devices.reshape(4, 2, 2, 4, 4, 2), ("x", "z1", "z0", "y", "zh", "c"))
    frames = P(("zh", "c"), None, None, EDGE_AXES, None)
    return jax.shard_map(
        local,
        mesh=split,
        in_specs=(frames, P(), P(), P(), P(), frames),
        out_specs=(frames, P(), P(), P(), P()),
        check_vma=False,
    )
```

```python
import functools
import math

import jax
import jax.numpy as jnp
from jax import lax
from jax.experimental import pallas as pl
from jax.experimental.pallas import tpu as pltpu
from jax.sharding import Mesh, PartitionSpec as P

BF = jnp.bfloat16
F32 = jnp.float32
C = 96
F = 5
W = 128
TAPS = 27
TPAD = 28
OPAD = 8
GROWS = TPAD * OPAD
HR = 4
FW = HR * W
POS = F * FW
KT = 9 * C
NW = TAPS * C
MAIN = 1920
TAIL = NW - MAIN
ROWS = 2048
EDGE_AXES = ("x", "z1", "z0", "y")
NEAR = ("x", "z0", "y", "c")
DEPTH = ("zh", "z1")
FAR = (((5, 0), (4, 1)), ((4, 0), (5, 1)))
SIDE = ((7, 6), (3, 2))
CLOSE = (((6, 1), (2, 0)), ((6, 0), (2, 1)), ((1, 0), (0, 1)))
SPREAD = (((0, 2), (1, 3)), ((1, 7), (3, 5)), ((2, 4), (7, 6)))


def nt(a, b):
    return lax.dot_general(a, b, (((1,), (1,)), ((), ())), preferred_element_type=F32)


def nn(a, b):
    return lax.dot_general(a, b, (((1,), (0,)), ((), ())), preferred_element_type=F32)


def tn(a, b):
    return lax.dot_general(a, b, (((0,), (0,)), ((), ())), preferred_element_type=F32)


def shifted(v, lane, by):
    if by == 0:
        return v
    if by > 0:
        return jnp.where(lane < W - 1, pltpu.roll(v, W - 1, 1), 0.0)
    return jnp.where(lane > 0, pltpu.roll(v, 1, 1), 0.0)


def flat_index(axes):
    index = 0
    for axis in axes:
        index = index * lax.axis_size(axis) + lax.axis_index(axis)
    return index


def device_kernel(
    n_rows, scale,
    own_ref, pair_ref, wt_ref, cb_ref, wo_ref, ob_ref, tgt_ref,
    dec_ref, pay_ref,
    q_ref, r_ref, hid_ref, fac_ref, y_ref, g_ref, gh_ref, main_ref,
):
    row_id = flat_index(EDGE_AXES)
    odd = lax.rem(row_id, 2)
    first = row_id == 0
    last = row_id == n_rows - 1
    lane96 = lax.broadcasted_iota(jnp.int32, (C, W), 1)
    lane8 = lax.broadcasted_iota(jnp.int32, (OPAD, W), 1)

    for g in range(F):
        for r in range(6):
            if r < 2:
                tile = pair_ref[1 - odd, g, r]
            elif r < 4:
                tile = own_ref[g, r - 2]
            else:
                tile = pair_ref[odd, g, r - 4]
            wide = tile.astype(F32)
            for kj in range(3):
                piece = tile if kj == 1 else shifted(wide, lane96, kj - 1).astype(BF)
                for ki in range(3):
                    i = r - ki
                    if 0 <= i < HR:
                        base = (ki * 3 + kj) * C
                        q_ref[base : base + C, g * FW + i * W : g * FW + (i + 1) * W] = piece

    srow = lax.broadcasted_iota(jnp.int32, (C, GROWS), 0)
    scol = lax.broadcasted_iota(jnp.int32, (C, GROWS), 1)
    pick = ((srow // 32 == scol % OPAD) & (srow % 32 == scol // OPAD)).astype(F32).astype(BF)
    wo = wo_ref[...]
    wo8 = tn(pick, wo).astype(BF)
    wo8t = tn(wo, pick).astype(BF)

    col = lax.broadcasted_iota(jnp.int32, (1, FW), 1)
    outside = ((col < W) & first) | ((col >= 3 * W) & last)
    keep = jnp.where(outside, 0.0, 1.0)
    def conv(f):
        low = max(0, f - 2) * C
        r_ref[f, low:, :] = nn(wt_ref[low:, :], q_ref[:, f * FW : (f + 1) * FW])

    def activate(f):
        pre = cb_ref[...]
        for kt in range(2, max(-1, 1 - f), -1):
            pre = pre + r_ref[f + kt - 2, kt * C : (kt + 1) * C, :]
        sig = jax.nn.sigmoid(pre)
        hid_ref[:, f * FW : (f + 1) * FW] = (pre * sig * keep).astype(BF)
        fac_ref[:, f * FW : (f + 1) * FW] = sig * (1.0 + pre * (1.0 - sig)) * keep

    def project(f):
        y_ref[:, f * FW : (f + 1) * FW] = nn(wo8, hid_ref[:, f * FW : (f + 1) * FW])

    for f in range(F + 2):
        if f < F:
            conv(f)
        if 1 <= f <= F:
            activate(f - 1)
        if f >= 2:
            project(f - 2)

    grads = {}
    obsum = jnp.zeros((OPAD, W), F32)
    for f in range(F):
        decs = []
        for i in range(2):
            dec = None
            for kj in range(3):
                z = None
                for kt in range(3):
                    g = f + kt - 2
                    if g < 0:
                        continue
                    for ki in range(3):
                        t = kt * 9 + ki * 3 + kj
                        at = g * FW + (i + ki) * W
                        v = y_ref[t * OPAD : (t + 1) * OPAD, at : at + W]
                        z = v if z is None else z + v
                z = shifted(z, lane8, kj - 1)
                dec = z if dec is None else dec + z
            dec = (dec + ob_ref[...]).astype(BF)
            at = (f * 2 + i) * W
            decs.append(dec.astype(F32))
            gf = ((dec.astype(F32) - tgt_ref[:, at : at + W]) * scale).astype(BF).astype(F32)
            obsum = obsum + gf
            for kj in range(3):
                grads[f, i, kj] = shifted(gf, lane8, 1 - kj)
        for o in range(3):
            rows = jnp.concatenate([d[o : o + 1] for d in decs], axis=0)
            dec_ref[0, o, f] = rows.astype(BF)

    none = jnp.zeros((OPAD, W), F32)
    for g in range(F):
        for i in range(HR):
            parts = []
            for t in range(TPAD):
                kt, ki, kj = t // 9, t // 3 % 3, t % 3
                parts.append(grads.get((g + 2 - kt, i - ki, kj), none) if t < TAPS else none)
            at = g * FW + i * W
            for p in range(TPAD // 2):
                both = jnp.concatenate(parts[2 * p : 2 * p + 2], axis=0).astype(BF)
                g_ref[p * 16 : (p + 1) * 16, at : at + W] = both

    gh_ref[C:W, :] = jnp.zeros((W - C, POS), BF)
    gh_ref[W + C :, :] = jnp.zeros((W - C, POS), BF)
    gh_ref[W:, POS - FW :] = jnp.zeros((W, FW), BF)
    for f in range(F):
        back = nn(wo8t, g_ref[:, f * FW : (f + 1) * FW])
        gh = (back * fac_ref[:, f * FW : (f + 1) * FW]).astype(BF)
        gh_ref[:C, f * FW : (f + 1) * FW] = gh
        if f:
            gh_ref[W : W + C, (f - 1) * FW : f * FW] = gh

    both = nt(q_ref[...], gh_ref[...])
    main_ref[2 * KT :, :] = both[:, :W]
    main_ref[KT : 2 * KT, :] = both[:, W:]
    main_ref[:KT, :] = nt(q_ref[:, : 3 * FW], gh_ref[:W, 2 * FW :])
    gow = nt(g_ref[...], hid_ref[...]).astype(BF)
    gow = nn(pick, gow)
    bias = nt(jnp.ones((OPAD, POS), BF), gh_ref[:W, :])
    obias = jnp.broadcast_to(jnp.sum(obsum, axis=1, keepdims=True), (OPAD, W))

    lane = lax.broadcasted_iota(jnp.int32, (TAIL, W), 1)
    for k in range(3):
        lo, hi = k * TAIL, (k + 1) * TAIL
        tail = pltpu.roll(main_ref[MAIN:, :], 96 - 32 * k, 1)
        if hi <= MAIN:
            head = main_ref[lo:hi, :]
        else:
            head = jnp.concatenate(
                [main_ref[lo:MAIN, :], jnp.pad(gow, ((0, 0), (0, W - C)))], axis=0
            )
        pay_ref[lo:hi, :] = jnp.where(lane < C, head, tail).astype(BF)
    for at, v in ((2016, bias), (2032, obias)):
        top = v.astype(BF).astype(F32)
        pay_ref[at : at + 16, :] = jnp.concatenate([top, v - top], axis=0).astype(BF)


def split_sums(total, is_last):
    out = total.astype(BF)
    start = total.shape[0] - 32
    fixed = []
    for at in (start, start + 16):
        whole = total[at : at + 8] + total[at + 8 : at + 16]
        top = whole.astype(BF).astype(F32)
        fixed += [top, whole - top]
    special = jnp.concatenate(([total[:start]] if start else []) + fixed, axis=0).astype(BF)
    return jnp.where(is_last, special, out)


def in_last():
    return flat_index(NEAR) == math.prod(lax.axis_size(a) for a in NEAR) - 1


def pass_on(value, pairs):
    outer, inner = (lax.axis_size(a) for a in DEPTH)
    place = [(d % inner) * outer + d // inner for d in range(outer * inner)]
    return lax.ppermute(value, DEPTH[::-1], [(place[i], place[j]) for i, j in pairs])


def plane_sum_kernel(in_ref, out_ref):
    total = in_ref[0].astype(F32)
    for k in range(1, in_ref.shape[0]):
        total = total + in_ref[k].astype(F32)
    out_ref[...] = split_sums(total, in_last())


def depth_sum_kernel(*refs):
    *in_refs, out_ref = refs
    total = in_refs[0][...].astype(F32)
    for ref in in_refs[1:]:
        total = total + ref[...].astype(F32)
    out_ref[...] = jnp.where(flat_index(DEPTH) < 2, split_sums(total, in_last()), jnp.zeros_like(out_ref))


def side_sum_kernel(part_ref, side_ref, out_ref):
    total = part_ref[...].astype(F32) + side_ref[...].astype(F32)
    at = flat_index(DEPTH)
    out_ref[...] = jnp.where((at == 2) | (at == 6), split_sums(total, in_last()), part_ref[...])


def copies_kernel(one_ref, two_ref, out_ref):
    either = one_ref[...] + two_ref[...]
    for k in range(out_ref.shape[0]):
        out_ref[k] = either


def unpack_kernel(in_ref, gw_ref, gb_ref, go_ref, gob_ref):
    def get(lo, hi):
        return in_ref[lo:hi, :].astype(F32)

    gw_ref[:MAIN, :] = get(0, MAIN)[:, :C]
    lane = lax.broadcasted_iota(jnp.int32, (TAIL, W), 1)
    tail = None
    for k in range(3):
        v = pltpu.roll(get(k * TAIL, (k + 1) * TAIL), 32 + 32 * k, 1)
        tail = v if tail is None else jnp.where(lane < 32 * k, tail, v)
    gw_ref[MAIN:, :] = tail[:, :C]
    gow = get(MAIN, MAIN + 96)
    for o in range(3):
        go_ref[o] = gow[o * 32 : o * 32 + TAPS, :C]
    sums = get(2016, 2048)
    gb_ref[...] = (sums[0:8] + sums[8:16])[0, :C]
    ob = sums[16:24] + sums[24:32]
    r8 = lax.broadcasted_iota(jnp.int32, (OPAD, W), 0)
    l8 = lax.broadcasted_iota(jnp.int32, (OPAD, W), 1)
    gob_ref[...] = jnp.sum(jnp.where(r8 == l8, ob, 0.0), axis=0)[:3]


VM = functools.partial(pl.BlockSpec, memory_space=pltpu.VMEM)
LIMIT = 48 * 1024 * 1024
SMALL = 4 * 1024 * 1024


def k1_call(n_rows, scale):
    return pl.pallas_call(
        functools.partial(device_kernel, n_rows, scale),
        out_shape=(
            jax.ShapeDtypeStruct((1, 3, F, 2, W), BF),
            jax.ShapeDtypeStruct((ROWS, W), BF),
        ),
        in_specs=[VM()] * 7,
        out_specs=(VM(), VM()),
        scratch_shapes=[
            pltpu.VMEM((KT, POS), BF),
            pltpu.VMEM((F, 3 * C, FW), F32),
            pltpu.VMEM((C, POS), BF),
            pltpu.VMEM((C, POS), F32),
            pltpu.VMEM((GROWS, POS), F32),
            pltpu.VMEM((GROWS, POS), BF),
            pltpu.VMEM((2 * W, POS), BF),
            pltpu.VMEM((NW, W), F32),
        ],
        compiler_params=pltpu.CompilerParams(vmem_limit_bytes=LIMIT),
        name="device_part",
    )


def local(latent_features, conv_weight, conv_bias, out_weight, out_bias, target_frames):
    sizes = [lax.axis_size(a) for a in EDGE_AXES]
    n_rows = math.prod(sizes)
    clips = lax.axis_size("zh") * lax.axis_size("c")
    scale = 1.0 / math.sqrt(3 * clips * F * 2 * n_rows * W)

    own = jnp.transpose(latent_features[0], (1, 2, 0, 3))
    even = [(i, i ^ 1) for i in range(n_rows)]
    odd = [(i, ((i + 1) ^ 1) - 1) for i in range(1, n_rows - 1)]
    pair = jnp.stack([lax.ppermute(own, EDGE_AXES, even), lax.ppermute(own, EDGE_AXES, odd)])

    wt = jnp.transpose(conv_weight.reshape(3, KT, C), (0, 2, 1)).reshape(3 * C, KT)
    wo = jnp.pad(jnp.transpose(out_weight, (2, 0, 1)), ((0, 0), (0, 5), (0, 0))).reshape(C, C)
    ob = jnp.pad(out_bias[:, None], ((0, 5), (0, 0)))
    tgt = jnp.pad(target_frames[0].reshape(3, F * 2 * W).astype(F32), ((0, 5), (0, 0)))

    decoded, packed = k1_call(n_rows, scale)(own, pair, wt, conv_bias[:, None], wo, ob, tgt)

    near = math.prod(lax.axis_size(a) for a in NEAR)
    chunk = ROWS // near

    def small(kernel, name, copies, *operands):
        return pl.pallas_call(
            kernel,
            out_shape=jax.ShapeDtypeStruct(copies + (chunk, W), BF),
            in_specs=[VM()] * len(operands),
            out_specs=VM(),
            compiler_params=pltpu.CompilerParams(vmem_limit_bytes=SMALL),
            name=name,
        )(*operands)

    parts = lax.all_to_all(packed.reshape(near, chunk, W), NEAR, 0, 0)
    part = small(plane_sum_kernel, "plane_sum", (), parts)
    side = pass_on(part, SIDE)
    more = small(side_sum_kernel, "side_sum", (), part, side)
    close = [pass_on(more, pairs) for pairs in CLOSE[::-1]]
    far = [pass_on(part, pairs) for pairs in FAR[::-1]]
    total = small(depth_sum_kernel, "depth_sum", (), part, *close, *far)
    for pairs in SPREAD[:-1]:
        total = total + pass_on(total, pairs)
    outer = pass_on(total, SPREAD[-1])
    parts = lax.all_to_all(small(copies_kernel, "copies", (near,), total, outer), NEAR, 0, 0)

    gw, gb, go, gob = pl.pallas_call(
        unpack_kernel,
        out_shape=(
            jax.ShapeDtypeStruct((NW, C), F32),
            jax.ShapeDtypeStruct((C,), F32),
            jax.ShapeDtypeStruct((3, TAPS, C), F32),
            jax.ShapeDtypeStruct((3,), F32),
        ),
        in_specs=[VM()],
        out_specs=(VM(),) * 4,
        compiler_params=pltpu.CompilerParams(vmem_limit_bytes=2 * SMALL),
        name="unpack",
    )(parts.reshape(ROWS, W))
    return (
        decoded,
        gw.reshape(TAPS, C, C),
        gb,
        jnp.transpose(go, (1, 2, 0)),
        gob,
    )


def solution(mesh):
    split = Mesh(mesh.devices.reshape(4, 2, 2, 4, 4, 2), ("x", "z1", "z0", "y", "zh", "c"))
    frames = P(("zh", "c"), None, None, EDGE_AXES, None)
    return jax.shard_map(
        local,
        mesh=split,
        in_specs=(frames, P(), P(), P(), P(), frames),
        out_specs=(frames, P(), P(), P(), P()),
        check_vma=False,
    )
```

```python
import functools
import math

import jax
import jax.numpy as jnp
from jax import lax
from jax.experimental import pallas as pl
from jax.experimental.pallas import tpu as pltpu
from jax.sharding import Mesh, PartitionSpec as P

BF = jnp.bfloat16
F32 = jnp.float32
C = 96
F = 5
W = 128
TAPS = 27
TPAD = 28
OPAD = 8
GROWS = TPAD * OPAD
HR = 4
FW = HR * W
POS = F * FW
KT = 9 * C
NW = TAPS * C
MAIN = 1920
TAIL = NW - MAIN
ROWS = 2048
AXES = ("x", "z1", "z0", "y", "zh", "c")
EDGE_AXES = ("x", "z1", "z0", "y")
NEAR = ("x", "z0", "y", "c")
DEPTH = ("zh", "z1")
FAR = (((5, 0), (4, 1)), ((4, 0), (5, 1)))
SIDE = ((7, 6), (3, 2))
CLOSE = (((6, 1), (2, 0)), ((6, 0), (2, 1)), ((1, 0), (0, 1)))
SPREAD = (((0, 2), (1, 3)), ((1, 7), (3, 5)), ((2, 4), (7, 6)))


def nt(a, b):
    return lax.dot_general(a, b, (((1,), (1,)), ((), ())), preferred_element_type=F32)


def nn(a, b):
    return lax.dot_general(a, b, (((1,), (0,)), ((), ())), preferred_element_type=F32)


def tn(a, b):
    return lax.dot_general(a, b, (((0,), (0,)), ((), ())), preferred_element_type=F32)


def shifted(v, lane, by):
    if by == 0:
        return v
    if by > 0:
        return jnp.where(lane < W - 1, pltpu.roll(v, W - 1, 1), 0.0)
    return jnp.where(lane > 0, pltpu.roll(v, 1, 1), 0.0)


FIRST = 33


def scatter_groups():
    nx, nz1, nz0, ny, nzh, nc = (lax.axis_size(a) for a in AXES)
    groups = []
    for z1 in range(nz1):
        for zh in range(nzh):
            members = []
            for place in range(nx * nz0 * ny * nc):
                rest, c = divmod(place ^ FIRST, nc)
                rest, y = divmod(rest, ny)
                x, z0 = divmod(rest, nz0)
                members.append(((((x * nz1 + z1) * nz0 + z0) * ny + y) * nzh + zh) * nc + c)
            groups.append(members)
    return groups


def flat_index(axes):
    index = 0
    for axis in axes:
        index = index * lax.axis_size(axis) + lax.axis_index(axis)
    return index


def device_kernel(
    n_rows, scale,
    own_ref, pair_ref, wt_ref, cb_ref, wo_ref, ob_ref, tgt_ref,
    dec_ref, out_ref,
    q_ref, r_ref, hid_ref, fac_ref, y_ref, g_ref, gh_ref, main_ref,
):
    row_id = flat_index(EDGE_AXES)
    odd = lax.rem(row_id, 2)
    first = row_id == 0
    last = row_id == n_rows - 1
    lane96 = lax.broadcasted_iota(jnp.int32, (C, W), 1)
    lane8 = lax.broadcasted_iota(jnp.int32, (OPAD, W), 1)

    q_ref[KT:, :] = jnp.ones((16, POS), BF)
    for g in range(F):
        for r in range(6):
            if r < 2:
                tile = pair_ref[1 - odd, g, r]
            elif r < 4:
                tile = own_ref[g, r - 2]
            else:
                tile = pair_ref[odd, g, r - 4]
            wide = tile.astype(F32)
            for kj in range(3):
                piece = tile if kj == 1 else shifted(wide, lane96, kj - 1).astype(BF)
                for ki in range(3):
                    i = r - ki
                    if 0 <= i < HR:
                        base = (ki * 3 + kj) * C
                        q_ref[base : base + C, g * FW + i * W : g * FW + (i + 1) * W] = piece

    srow = lax.broadcasted_iota(jnp.int32, (C, GROWS), 0)
    scol = lax.broadcasted_iota(jnp.int32, (C, GROWS), 1)
    pick = ((srow // 32 == scol % OPAD) & (srow % 32 == scol // OPAD)).astype(F32).astype(BF)
    wo = wo_ref[...]
    wo8 = tn(pick, wo).astype(BF)
    wo8t = tn(wo, pick).astype(BF)

    col = lax.broadcasted_iota(jnp.int32, (1, FW), 1)
    outside = ((col < W) & first) | ((col >= 3 * W) & last)
    keep = jnp.where(outside, 0.0, 1.0)
    def conv(f):
        low = max(0, f - 2) * C
        r_ref[f, low:, :] = nn(wt_ref[low:, :], q_ref[:KT, f * FW : (f + 1) * FW])

    def activate(f):
        pre = cb_ref[...]
        for kt in range(2, max(-1, 1 - f), -1):
            pre = pre + r_ref[f + kt - 2, kt * C : (kt + 1) * C, :]
        sig = jax.nn.sigmoid(pre)
        hid_ref[:, f * FW : (f + 1) * FW] = (pre * sig * keep).astype(BF)
        fac_ref[:, f * FW : (f + 1) * FW] = sig * (1.0 + pre * (1.0 - sig)) * keep

    def project(f):
        y_ref[:, f * FW : (f + 1) * FW] = nn(wo8, hid_ref[:, f * FW : (f + 1) * FW])

    for f in range(F + 2):
        if f < F:
            conv(f)
        if 1 <= f <= F:
            activate(f - 1)
        if f >= 2:
            project(f - 2)

    grads = {}
    obsum = jnp.zeros((OPAD, W), F32)
    for f in range(F):
        decs = []
        for i in range(2):
            dec = None
            for kj in range(3):
                z = None
                for kt in range(3):
                    g = f + kt - 2
                    if g < 0:
                        continue
                    for ki in range(3):
                        t = kt * 9 + ki * 3 + kj
                        at = g * FW + (i + ki) * W
                        v = y_ref[t * OPAD : (t + 1) * OPAD, at : at + W]
                        z = v if z is None else z + v
                z = shifted(z, lane8, kj - 1)
                dec = z if dec is None else dec + z
            dec = (dec + ob_ref[...]).astype(BF)
            at = (f * 2 + i) * W
            decs.append(dec.astype(F32))
            gf = ((dec.astype(F32) - tgt_ref[:, at : at + W]) * scale).astype(BF).astype(F32)
            obsum = obsum + gf
            for kj in range(3):
                grads[f, i, kj] = shifted(gf, lane8, 1 - kj)
        for o in range(3):
            rows = jnp.concatenate([d[o : o + 1] for d in decs], axis=0)
            dec_ref[0, o, f] = rows.astype(BF)

    none = jnp.zeros((OPAD, W), F32)
    for g in range(F):
        for i in range(HR):
            parts = []
            for t in range(TPAD):
                kt, ki, kj = t // 9, t // 3 % 3, t % 3
                parts.append(grads.get((g + 2 - kt, i - ki, kj), none) if t < TAPS else none)
            at = g * FW + i * W
            for p in range(TPAD // 2):
                both = jnp.concatenate(parts[2 * p : 2 * p + 2], axis=0).astype(BF)
                g_ref[p * 16 : (p + 1) * 16, at : at + W] = both

    gh_ref[C:W, :] = jnp.zeros((W - C, POS), BF)
    gh_ref[W + C :, :] = jnp.zeros((W - C, POS), BF)
    gh_ref[W:, POS - FW :] = jnp.zeros((W, FW), BF)
    for f in range(F):
        back = nn(wo8t, g_ref[:, f * FW : (f + 1) * FW])
        gh = (back * fac_ref[:, f * FW : (f + 1) * FW]).astype(BF)
        gh_ref[:C, f * FW : (f + 1) * FW] = gh
        if f:
            gh_ref[W : W + C, (f - 1) * FW : f * FW] = gh

    both = nt(q_ref[...], gh_ref[...])
    main_ref[2 * KT : NW, :] = both[:KT, :W]
    main_ref[NW:, :] = both[KT:, :W]
    main_ref[KT : 2 * KT, :] = both[:KT, W:]
    main_ref[:KT, :] = nt(q_ref[:KT, : 3 * FW], gh_ref[:W, 2 * FW :])
    gow = nt(g_ref[...], hid_ref[...]).astype(BF)
    gow = nn(pick, gow)
    bias = main_ref[NW : NW + OPAD, :]
    obias = jnp.broadcast_to(jnp.sum(obsum, axis=1, keepdims=True), (OPAD, W))

    lane = lax.broadcasted_iota(jnp.int32, (TAIL, W), 1)
    for k in range(3):
        lo, hi = k * TAIL, (k + 1) * TAIL
        tail = pltpu.roll(main_ref[MAIN:NW, :], 96 - 32 * k, 1)
        if hi <= MAIN:
            head = main_ref[lo:hi, :]
        else:
            head = jnp.concatenate(
                [main_ref[lo:MAIN, :], jnp.pad(gow, ((0, 0), (0, W - C)))], axis=0
            )
        out_ref[lo:hi, :] = jnp.where(lane < C, head, tail).astype(BF)
    ends = []
    for v in (bias, obias):
        top = v.astype(BF).astype(F32)
        ends += [top, v - top]
    out_ref[ROWS - 32 :, :] = jnp.concatenate(ends, axis=0).astype(BF)


def split_sums(total, is_last):
    out = total.astype(BF)
    start = total.shape[0] - 32
    fixed = []
    for at in (start, start + 16):
        whole = total[at : at + 8] + total[at + 8 : at + 16]
        top = whole.astype(BF).astype(F32)
        fixed += [top, whole - top]
    special = jnp.concatenate(([total[:start]] if start else []) + fixed, axis=0).astype(BF)
    return jnp.where(is_last, special, out)


def in_last():
    last = math.prod(lax.axis_size(a) for a in NEAR) - 1
    return flat_index(NEAR) == last ^ FIRST


def pass_on(value, pairs):
    outer, inner = (lax.axis_size(a) for a in DEPTH)
    place = [(d % inner) * outer + d // inner for d in range(outer * inner)]
    return lax.ppermute(value, DEPTH[::-1], [(place[i], place[j]) for i, j in pairs])


def plane_sum_kernel(in_ref, out_ref):
    total = in_ref[0].astype(F32)
    for k in range(1, in_ref.shape[0]):
        total = total + in_ref[k].astype(F32)
    out_ref[...] = split_sums(total, in_last())


def depth_sum_kernel(*refs):
    *in_refs, out_ref = refs
    total = in_refs[0][...].astype(F32)
    for ref in in_refs[1:]:
        total = total + ref[...].astype(F32)
    out_ref[...] = jnp.where(flat_index(DEPTH) < 2, split_sums(total, in_last()), jnp.zeros_like(out_ref))


def side_sum_kernel(part_ref, side_ref, out_ref):
    total = part_ref[...].astype(F32) + side_ref[...].astype(F32)
    at = flat_index(DEPTH)
    out_ref[...] = jnp.where((at == 2) | (at == 6), split_sums(total, in_last()), part_ref[...])


def copies_kernel(one_ref, two_ref, out_ref):
    either = one_ref[...] + two_ref[...]
    for k in range(out_ref.shape[0]):
        out_ref[k] = either


def unpack_kernel(in_ref, gw_ref, gb_ref, go_ref, gob_ref):
    def get(lo, hi):
        return in_ref[lo:hi, :].astype(F32)

    gw_ref[:MAIN, :] = get(0, MAIN)[:, :C]
    lane = lax.broadcasted_iota(jnp.int32, (TAIL, W), 1)
    tail = None
    for k in range(3):
        v = pltpu.roll(get(k * TAIL, (k + 1) * TAIL), 32 + 32 * k, 1)
        tail = v if tail is None else jnp.where(lane < 32 * k, tail, v)
    gw_ref[MAIN:, :] = tail[:, :C]
    gow = get(MAIN, MAIN + 96)
    for o in range(3):
        go_ref[o] = gow[o * 32 : o * 32 + TAPS, :C]
    sums = get(2016, 2048)
    gb_ref[...] = (sums[0:8] + sums[8:16])[0, :C]
    ob = sums[16:24] + sums[24:32]
    r8 = lax.broadcasted_iota(jnp.int32, (OPAD, W), 0)
    l8 = lax.broadcasted_iota(jnp.int32, (OPAD, W), 1)
    gob_ref[...] = jnp.sum(jnp.where(r8 == l8, ob, 0.0), axis=0)[:3]


VM = functools.partial(pl.BlockSpec, memory_space=pltpu.VMEM)
LIMIT = 48 * 1024 * 1024
SMALL = 4 * 1024 * 1024


def k1_call(n_rows, scale):
    return pl.pallas_call(
        functools.partial(device_kernel, n_rows, scale),
        out_shape=(
            jax.ShapeDtypeStruct((1, 3, F, 2, W), BF),
            jax.ShapeDtypeStruct((ROWS, W), BF),
        ),
        in_specs=[VM()] * 7,
        out_specs=(VM(), VM()),
        scratch_shapes=[
            pltpu.VMEM((KT + 16, POS), BF),
            pltpu.VMEM((F, 3 * C, FW), F32),
            pltpu.VMEM((C, POS), BF),
            pltpu.VMEM((C, POS), F32),
            pltpu.VMEM((GROWS, POS), F32),
            pltpu.VMEM((GROWS, POS), BF),
            pltpu.VMEM((2 * W, POS), BF),
            pltpu.VMEM((NW + 16, W), F32),
        ],
        compiler_params=pltpu.CompilerParams(vmem_limit_bytes=LIMIT),
        name="device_part",
    )


def local(latent_features, conv_weight, conv_bias, out_weight, out_bias, target_frames):
    sizes = [lax.axis_size(a) for a in EDGE_AXES]
    n_rows = math.prod(sizes)
    near = math.prod(lax.axis_size(a) for a in NEAR)
    clips = lax.axis_size("zh") * lax.axis_size("c")
    scale = 1.0 / math.sqrt(3 * clips * F * 2 * n_rows * W)

    own = jnp.transpose(latent_features[0], (1, 2, 0, 3))
    even = [(i, i ^ 1) for i in range(n_rows)]
    odd = [(i, ((i + 1) ^ 1) - 1) for i in range(1, n_rows - 1)]
    pair = jnp.stack([lax.ppermute(own, EDGE_AXES, even), lax.ppermute(own, EDGE_AXES, odd)])

    wt = jnp.transpose(conv_weight.reshape(3, KT, C), (0, 2, 1)).reshape(3 * C, KT)
    wo = jnp.pad(jnp.transpose(out_weight, (2, 0, 1)), ((0, 0), (0, 5), (0, 0))).reshape(C, C)
    ob = jnp.pad(out_bias[:, None], ((0, 5), (0, 0)))
    tgt = jnp.pad(target_frames[0].reshape(3, F * 2 * W).astype(F32), ((0, 5), (0, 0)))

    decoded, packed = k1_call(n_rows, scale)(own, pair, wt, conv_bias[:, None], wo, ob, tgt)

    chunk = ROWS // near

    def small(kernel, name, copies, *operands):
        return pl.pallas_call(
            kernel,
            out_shape=jax.ShapeDtypeStruct(copies + (chunk, W), BF),
            in_specs=[VM()] * len(operands),
            out_specs=VM(),
            compiler_params=pltpu.CompilerParams(vmem_limit_bytes=SMALL),
            name=name,
        )(*operands)

    parts = lax.all_to_all(packed.reshape(near, chunk, W), AXES, 0, 0, axis_index_groups=scatter_groups())
    part = small(plane_sum_kernel, "plane_sum", (), parts)
    side = pass_on(part, SIDE)
    more = small(side_sum_kernel, "side_sum", (), part, side)
    close = [pass_on(more, pairs) for pairs in CLOSE[::-1]]
    far = [pass_on(part, pairs) for pairs in FAR[::-1]]
    total = small(depth_sum_kernel, "depth_sum", (), part, *close, *far)
    for pairs in SPREAD[:-1]:
        total = total + pass_on(total, pairs)
    outer = pass_on(total, SPREAD[-1])
    parts = small(copies_kernel, "copies", (near,), total, outer)
    parts = lax.all_to_all(parts, AXES, 0, 0, axis_index_groups=scatter_groups())

    gw, gb, go, gob = pl.pallas_call(
        unpack_kernel,
        out_shape=(
            jax.ShapeDtypeStruct((NW, C), F32),
            jax.ShapeDtypeStruct((C,), F32),
            jax.ShapeDtypeStruct((3, TAPS, C), F32),
            jax.ShapeDtypeStruct((3,), F32),
        ),
        in_specs=[VM()],
        out_specs=(VM(),) * 4,
        compiler_params=pltpu.CompilerParams(vmem_limit_bytes=2 * SMALL),
        name="unpack",
    )(parts.reshape(ROWS, W))
    return (
        decoded,
        gw.reshape(TAPS, C, C),
        gb,
        jnp.transpose(go, (1, 2, 0)),
        gob,
    )


def solution(mesh):
    split = Mesh(mesh.devices.reshape(4, 2, 2, 4, 4, 2), AXES)
    frames = P(("zh", "c"), None, None, EDGE_AXES, None)
    return jax.shard_map(
        local,
        mesh=split,
        in_specs=(frames, P(), P(), P(), P(), frames),
        out_specs=(frames, P(), P(), P(), P()),
        check_vma=False,
    )
```

```python
import functools
import math

import jax
import jax.numpy as jnp
from jax import lax
from jax.experimental import pallas as pl
from jax.experimental.pallas import tpu as pltpu
from jax.sharding import Mesh, PartitionSpec as P

BF = jnp.bfloat16
F32 = jnp.float32
C = 96
F = 5
W = 128
TAPS = 27
TPAD = 28
OPAD = 8
GROWS = TPAD * OPAD
HR = 4
FW = HR * W
POS = F * FW
KT = 9 * C
NW = TAPS * C
MAIN = 1920
TAIL = NW - MAIN
ROWS = 2048
AXES = ("x", "z1", "z0", "y", "zh", "c")
EDGE_AXES = ("x", "z1", "z0", "y")
NEAR = ("x", "z0", "y", "c")
DEPTH = ("zh", "z1")
FAR = (((5, 0), (4, 1)), ((4, 0), (5, 1)))
SIDE = ((7, 6), (3, 2))
CLOSE = (((6, 1), (2, 0)), ((6, 0), (2, 1)), ((1, 0), (0, 1)))
SPREAD = (((0, 2), (1, 3)), ((1, 7), (3, 5)), ((2, 4), (7, 6)))


def nt(a, b):
    return lax.dot_general(a, b, (((1,), (1,)), ((), ())), preferred_element_type=F32)


def nn(a, b):
    return lax.dot_general(a, b, (((1,), (0,)), ((), ())), preferred_element_type=F32)


def tn(a, b):
    return lax.dot_general(a, b, (((0,), (0,)), ((), ())), preferred_element_type=F32)


def shifted(v, lane, by):
    if by == 0:
        return v
    if by > 0:
        return jnp.where(lane < W - 1, pltpu.roll(v, W - 1, 1), 0.0)
    return jnp.where(lane > 0, pltpu.roll(v, 1, 1), 0.0)


FIRST = 41


def scatter_groups():
    nx, nz1, nz0, ny, nzh, nc = (lax.axis_size(a) for a in AXES)
    groups = []
    for z1 in range(nz1):
        for zh in range(nzh):
            members = []
            for place in range(nx * nz0 * ny * nc):
                rest, c = divmod(place ^ FIRST, nc)
                rest, y = divmod(rest, ny)
                x, z0 = divmod(rest, nz0)
                members.append(((((x * nz1 + z1) * nz0 + z0) * ny + y) * nzh + zh) * nc + c)
            groups.append(members)
    return groups


def flat_index(axes):
    index = 0
    for axis in axes:
        index = index * lax.axis_size(axis) + lax.axis_index(axis)
    return index


def device_kernel(
    n_rows, scale,
    own_ref, one_ref, two_ref, wt_ref, cb_ref, wo_ref, ob_ref, tgt_ref,
    dec_ref, out_ref,
    q_ref, r_ref, hid_ref, fac_ref, y_ref, g_ref, gh_ref, main_ref,
):
    row_id = flat_index(EDGE_AXES)
    prev_first = lax.rem(row_id + lax.axis_index("c"), 2) == 1
    first = row_id == 0
    last = row_id == n_rows - 1
    lane96 = lax.broadcasted_iota(jnp.int32, (C, W), 1)
    lane8 = lax.broadcasted_iota(jnp.int32, (OPAD, W), 1)

    q_ref[KT:, :] = jnp.ones((16, POS), BF)
    for g in range(F):
        for r in range(6):
            if r < 2:
                tile = jnp.where(prev_first, one_ref[g, r], two_ref[g, r])
            elif r < 4:
                tile = own_ref[g, r - 2]
            else:
                tile = jnp.where(prev_first, two_ref[g, r - 4], one_ref[g, r - 4])
            wide = tile.astype(F32)
            for kj in range(3):
                piece = tile if kj == 1 else shifted(wide, lane96, kj - 1).astype(BF)
                for ki in range(3):
                    i = r - ki
                    if 0 <= i < HR:
                        base = (ki * 3 + kj) * C
                        q_ref[base : base + C, g * FW + i * W : g * FW + (i + 1) * W] = piece

    srow = lax.broadcasted_iota(jnp.int32, (C, GROWS), 0)
    scol = lax.broadcasted_iota(jnp.int32, (C, GROWS), 1)
    pick = ((srow // 32 == scol % OPAD) & (srow % 32 == scol // OPAD)).astype(F32).astype(BF)
    wo = wo_ref[...]
    wo8 = tn(pick, wo).astype(BF)
    wo8t = tn(wo, pick).astype(BF)

    col = lax.broadcasted_iota(jnp.int32, (1, FW), 1)
    outside = ((col < W) & first) | ((col >= 3 * W) & last)
    keep = jnp.where(outside, 0.0, 1.0)
    def conv(f):
        low = max(0, f - 2) * C
        r_ref[f, low:, :] = nn(wt_ref[low:, :], q_ref[:KT, f * FW : (f + 1) * FW])

    def activate(f):
        pre = cb_ref[...]
        for kt in range(2, max(-1, 1 - f), -1):
            pre = pre + r_ref[f + kt - 2, kt * C : (kt + 1) * C, :]
        sig = jax.nn.sigmoid(pre)
        hid_ref[:, f * FW : (f + 1) * FW] = (pre * sig * keep).astype(BF)
        fac_ref[:, f * FW : (f + 1) * FW] = sig * (1.0 + pre * (1.0 - sig)) * keep

    def project(f):
        y_ref[:, f * FW : (f + 1) * FW] = nn(wo8, hid_ref[:, f * FW : (f + 1) * FW])

    for f in range(F + 2):
        if f < F:
            conv(f)
        if 1 <= f <= F:
            activate(f - 1)
        if f >= 2:
            project(f - 2)

    grads = {}
    obsum = jnp.zeros((OPAD, W), F32)
    for f in range(F):
        decs = []
        for i in range(2):
            dec = None
            for kj in range(3):
                z = None
                for kt in range(3):
                    g = f + kt - 2
                    if g < 0:
                        continue
                    for ki in range(3):
                        t = kt * 9 + ki * 3 + kj
                        at = g * FW + (i + ki) * W
                        v = y_ref[t * OPAD : (t + 1) * OPAD, at : at + W]
                        z = v if z is None else z + v
                z = shifted(z, lane8, kj - 1)
                dec = z if dec is None else dec + z
            dec = (dec + ob_ref[...]).astype(BF)
            at = (f * 2 + i) * W
            decs.append(dec.astype(F32))
            gf = ((dec.astype(F32) - tgt_ref[:, at : at + W]) * scale).astype(BF).astype(F32)
            obsum = obsum + gf
            for kj in range(3):
                grads[f, i, kj] = shifted(gf, lane8, 1 - kj)
        for o in range(3):
            rows = jnp.concatenate([d[o : o + 1] for d in decs], axis=0)
            dec_ref[0, o, f] = rows.astype(BF)

    none = jnp.zeros((OPAD, W), F32)
    for g in range(F):
        for i in range(HR):
            parts = []
            for t in range(TPAD):
                kt, ki, kj = t // 9, t // 3 % 3, t % 3
                parts.append(grads.get((g + 2 - kt, i - ki, kj), none) if t < TAPS else none)
            at = g * FW + i * W
            for p in range(TPAD // 2):
                both = jnp.concatenate(parts[2 * p : 2 * p + 2], axis=0).astype(BF)
                g_ref[p * 16 : (p + 1) * 16, at : at + W] = both

    gh_ref[C:W, :] = jnp.zeros((W - C, POS), BF)
    gh_ref[W + C :, :] = jnp.zeros((W - C, POS), BF)
    gh_ref[W:, POS - FW :] = jnp.zeros((W, FW), BF)
    for f in range(F):
        back = nn(wo8t, g_ref[:, f * FW : (f + 1) * FW])
        gh = (back * fac_ref[:, f * FW : (f + 1) * FW]).astype(BF)
        gh_ref[:C, f * FW : (f + 1) * FW] = gh
        if f:
            gh_ref[W : W + C, (f - 1) * FW : f * FW] = gh

    both = nt(q_ref[...], gh_ref[...])
    main_ref[2 * KT : NW, :] = both[:KT, :W]
    main_ref[NW:, :] = both[KT:, :W]
    main_ref[KT : 2 * KT, :] = both[:KT, W:]
    main_ref[:KT, :] = nt(q_ref[:KT, : 3 * FW], gh_ref[:W, 2 * FW :])
    gow = nt(g_ref[...], hid_ref[...]).astype(BF)
    gow = nn(pick, gow)
    bias = main_ref[NW : NW + OPAD, :]
    obias = jnp.broadcast_to(jnp.sum(obsum, axis=1, keepdims=True), (OPAD, W))

    lane = lax.broadcasted_iota(jnp.int32, (TAIL, W), 1)
    for k in range(3):
        lo, hi = k * TAIL, (k + 1) * TAIL
        tail = pltpu.roll(main_ref[MAIN:NW, :], 96 - 32 * k, 1)
        if hi <= MAIN:
            head = main_ref[lo:hi, :]
        else:
            head = jnp.concatenate(
                [main_ref[lo:MAIN, :], jnp.pad(gow, ((0, 0), (0, W - C)))], axis=0
            )
        out_ref[lo:hi, :] = jnp.where(lane < C, head, tail).astype(BF)
    ends = []
    for v in (bias, obias):
        top = v.astype(BF).astype(F32)
        ends += [top, v - top]
    out_ref[ROWS - 32 :, :] = jnp.concatenate(ends, axis=0).astype(BF)


def split_sums(total, is_last):
    out = total.astype(BF)
    start = total.shape[0] - 32
    fixed = []
    for at in (start, start + 16):
        whole = total[at : at + 8] + total[at + 8 : at + 16]
        top = whole.astype(BF).astype(F32)
        fixed += [top, whole - top]
    special = jnp.concatenate(([total[:start]] if start else []) + fixed, axis=0).astype(BF)
    return jnp.where(is_last, special, out)


def in_last():
    last = math.prod(lax.axis_size(a) for a in NEAR) - 1
    return flat_index(NEAR) == last ^ FIRST


def pass_on(value, pairs):
    outer, inner = (lax.axis_size(a) for a in DEPTH)
    place = [(d % inner) * outer + d // inner for d in range(outer * inner)]
    return lax.ppermute(value, DEPTH[::-1], [(place[i], place[j]) for i, j in pairs])


def plane_sum_kernel(in_ref, out_ref):
    total = in_ref[0].astype(F32)
    for k in range(1, in_ref.shape[0]):
        total = total + in_ref[k].astype(F32)
    out_ref[...] = split_sums(total, in_last())


def depth_sum_kernel(*refs):
    *in_refs, out_ref = refs
    total = in_refs[0][...].astype(F32)
    for ref in in_refs[1:]:
        total = total + ref[...].astype(F32)
    out_ref[...] = jnp.where(flat_index(DEPTH) < 2, split_sums(total, in_last()), jnp.zeros_like(out_ref))


def side_sum_kernel(part_ref, side_ref, out_ref):
    total = part_ref[...].astype(F32) + side_ref[...].astype(F32)
    at = flat_index(DEPTH)
    out_ref[...] = jnp.where((at == 2) | (at == 6), split_sums(total, in_last()), part_ref[...])


def copies_kernel(one_ref, two_ref, out_ref):
    either = one_ref[...] + two_ref[...]
    for k in range(out_ref.shape[0]):
        out_ref[k] = either


def unpack_kernel(in_ref, gw_ref, gb_ref, go_ref, gob_ref):
    def get(lo, hi):
        return in_ref[lo:hi, :].astype(F32)

    gw_ref[:MAIN, :] = get(0, MAIN)[:, :C]
    lane = lax.broadcasted_iota(jnp.int32, (TAIL, W), 1)
    tail = None
    for k in range(3):
        v = pltpu.roll(get(k * TAIL, (k + 1) * TAIL), 32 + 32 * k, 1)
        tail = v if tail is None else jnp.where(lane < 32 * k, tail, v)
    gw_ref[MAIN:, :] = tail[:, :C]
    gow = get(MAIN, MAIN + 96)
    for o in range(3):
        go_ref[o] = gow[o * 32 : o * 32 + TAPS, :C]
    sums = get(2016, 2048)
    gb_ref[...] = (sums[0:8] + sums[8:16])[0, :C]
    ob = sums[16:24] + sums[24:32]
    r8 = lax.broadcasted_iota(jnp.int32, (OPAD, W), 0)
    l8 = lax.broadcasted_iota(jnp.int32, (OPAD, W), 1)
    gob_ref[...] = jnp.sum(jnp.where(r8 == l8, ob, 0.0), axis=0)[:3]


VM = functools.partial(pl.BlockSpec, memory_space=pltpu.VMEM)
LIMIT = 48 * 1024 * 1024
SMALL = 4 * 1024 * 1024


def k1_call(n_rows, scale):
    return pl.pallas_call(
        functools.partial(device_kernel, n_rows, scale),
        out_shape=(
            jax.ShapeDtypeStruct((1, 3, F, 2, W), BF),
            jax.ShapeDtypeStruct((ROWS, W), BF),
        ),
        in_specs=[VM()] * 8,
        out_specs=(VM(), VM()),
        scratch_shapes=[
            pltpu.VMEM((KT + 16, POS), BF),
            pltpu.VMEM((F, 3 * C, FW), F32),
            pltpu.VMEM((C, POS), BF),
            pltpu.VMEM((C, POS), F32),
            pltpu.VMEM((GROWS, POS), F32),
            pltpu.VMEM((GROWS, POS), BF),
            pltpu.VMEM((2 * W, POS), BF),
            pltpu.VMEM((NW + 16, W), F32),
        ],
        compiler_params=pltpu.CompilerParams(vmem_limit_bytes=LIMIT),
        name="device_part",
    )


def local(latent_features, conv_weight, conv_bias, out_weight, out_bias, target_frames):
    sizes = [lax.axis_size(a) for a in EDGE_AXES]
    n_rows = math.prod(sizes)
    near = math.prod(lax.axis_size(a) for a in NEAR)
    clips = lax.axis_size("zh") * lax.axis_size("c")
    scale = 1.0 / math.sqrt(3 * clips * F * 2 * n_rows * W)

    own = jnp.transpose(latent_features[0], (1, 2, 0, 3))
    even = [(i, i ^ 1) for i in range(n_rows)]
    odd = [(i, ((i + 1) ^ 1) - 1) for i in range(1, n_rows - 1)]
    axes = EDGE_AXES + ("c",)
    one = lax.ppermute(own, axes, [(2 * i, 2 * j) for i, j in even] + [(2 * i + 1, 2 * j + 1) for i, j in odd])
    two = lax.ppermute(own, axes, [(2 * i, 2 * j) for i, j in odd] + [(2 * i + 1, 2 * j + 1) for i, j in even])

    wt = jnp.transpose(conv_weight.reshape(3, KT, C), (0, 2, 1)).reshape(3 * C, KT)
    wo = jnp.pad(jnp.transpose(out_weight, (2, 0, 1)), ((0, 0), (0, 5), (0, 0))).reshape(C, C)
    ob = jnp.pad(out_bias[:, None], ((0, 5), (0, 0)))
    tgt = jnp.pad(target_frames[0].reshape(3, F * 2 * W).astype(F32), ((0, 5), (0, 0)))

    decoded, packed = k1_call(n_rows, scale)(own, one, two, wt, conv_bias[:, None], wo, ob, tgt)

    chunk = ROWS // near

    def small(kernel, name, copies, *operands):
        return pl.pallas_call(
            kernel,
            out_shape=jax.ShapeDtypeStruct(copies + (chunk, W), BF),
            in_specs=[VM()] * len(operands),
            out_specs=VM(),
            compiler_params=pltpu.CompilerParams(vmem_limit_bytes=SMALL),
            name=name,
        )(*operands)

    parts = lax.all_to_all(packed.reshape(near, chunk, W), AXES, 0, 0, axis_index_groups=scatter_groups())
    part = small(plane_sum_kernel, "plane_sum", (), parts)
    side = pass_on(part, SIDE)
    more = small(side_sum_kernel, "side_sum", (), part, side)
    close = [pass_on(more, pairs) for pairs in CLOSE[::-1]]
    far = [pass_on(part, pairs) for pairs in FAR[::-1]]
    total = small(depth_sum_kernel, "depth_sum", (), part, *close, *far)
    for pairs in SPREAD[:-1]:
        total = total + pass_on(total, pairs)
    outer = pass_on(total, SPREAD[-1])
    parts = small(copies_kernel, "copies", (near,), total, outer)
    parts = lax.all_to_all(parts, AXES, 0, 0, axis_index_groups=scatter_groups())

    gw, gb, go, gob = pl.pallas_call(
        unpack_kernel,
        out_shape=(
            jax.ShapeDtypeStruct((NW, C), F32),
            jax.ShapeDtypeStruct((C,), F32),
            jax.ShapeDtypeStruct((3, TAPS, C), F32),
            jax.ShapeDtypeStruct((3,), F32),
        ),
        in_specs=[VM()],
        out_specs=(VM(),) * 4,
        compiler_params=pltpu.CompilerParams(vmem_limit_bytes=2 * SMALL),
        name="unpack",
    )(parts.reshape(ROWS, W))
    return (
        decoded,
        gw.reshape(TAPS, C, C),
        gb,
        jnp.transpose(go, (1, 2, 0)),
        gob,
    )


def solution(mesh):
    split = Mesh(mesh.devices.reshape(4, 2, 2, 4, 4, 2), AXES)
    frames = P(("zh", "c"), None, None, EDGE_AXES, None)
    return jax.shard_map(
        local,
        mesh=split,
        in_specs=(frames, P(), P(), P(), P(), frames),
        out_specs=(frames, P(), P(), P(), P()),
        check_vma=False,
    )
```

```python
import functools
import math

import jax
import jax.numpy as jnp
from jax import lax
from jax.experimental import pallas as pl
from jax.experimental.pallas import tpu as pltpu
from jax.sharding import Mesh, PartitionSpec as P

BF = jnp.bfloat16
F32 = jnp.float32
C = 96
F = 5
W = 128
TAPS = 27
TPAD = 28
OPAD = 8
GROWS = TPAD * OPAD
HR = 4
FW = HR * W
POS = F * FW
KT = 9 * C
NW = TAPS * C
MAIN = 1920
TAIL = NW - MAIN
ROWS = 2048
AXES = ("x", "z1", "z0", "y", "zh", "c")
EDGE_AXES = ("x", "z1", "z0", "y")
NEAR = ("x", "z0", "y", "c")
DEPTH = ("zh", "z1")
FAR = (((5, 0), (4, 1)), ((4, 0), (5, 1)))
SIDE = ((7, 6), (3, 2))
CLOSE = (((6, 1), (2, 0)), ((6, 0), (2, 1)), ((1, 0), (0, 1)))
SPREAD = (((0, 2), (1, 3)), ((1, 7),), ((2, 4), (3, 5), (7, 6)))


def nt(a, b):
    return lax.dot_general(a, b, (((1,), (1,)), ((), ())), preferred_element_type=F32)


def nn(a, b):
    return lax.dot_general(a, b, (((1,), (0,)), ((), ())), preferred_element_type=F32)


def tn(a, b):
    return lax.dot_general(a, b, (((0,), (0,)), ((), ())), preferred_element_type=F32)


def shifted(v, lane, by):
    if by == 0:
        return v
    if by > 0:
        return jnp.where(lane < W - 1, pltpu.roll(v, W - 1, 1), 0.0)
    return jnp.where(lane > 0, pltpu.roll(v, 1, 1), 0.0)


FIRST = 41


def scatter_groups():
    nx, nz1, nz0, ny, nzh, nc = (lax.axis_size(a) for a in AXES)
    groups = []
    for z1 in range(nz1):
        for zh in range(nzh):
            members = []
            for place in range(nx * nz0 * ny * nc):
                rest, c = divmod(place ^ FIRST, nc)
                rest, y = divmod(rest, ny)
                x, z0 = divmod(rest, nz0)
                members.append(((((x * nz1 + z1) * nz0 + z0) * ny + y) * nzh + zh) * nc + c)
            groups.append(members)
    return groups


def flat_index(axes):
    index = 0
    for axis in axes:
        index = index * lax.axis_size(axis) + lax.axis_index(axis)
    return index


def device_kernel(
    n_rows, scale,
    own_ref, one_ref, two_ref, wt_ref, cb_ref, wo_ref, ob_ref, tgt_ref,
    dec_ref, out_ref,
    q_ref, r_ref, hid_ref, fac_ref, y_ref, g_ref, gh_ref, main_ref,
):
    row_id = flat_index(EDGE_AXES)
    prev_first = lax.rem(row_id + lax.axis_index("c"), 2) == 1
    first = row_id == 0
    last = row_id == n_rows - 1
    lane96 = lax.broadcasted_iota(jnp.int32, (C, W), 1)
    lane8 = lax.broadcasted_iota(jnp.int32, (OPAD, W), 1)

    q_ref[KT:, :] = jnp.ones((16, POS), BF)
    for g in range(F):
        for r in range(6):
            if r < 2:
                tile = jnp.where(prev_first, one_ref[g, r], two_ref[g, r])
            elif r < 4:
                tile = own_ref[g, r - 2]
            else:
                tile = jnp.where(prev_first, two_ref[g, r - 4], one_ref[g, r - 4])
            wide = tile.astype(F32)
            for kj in range(3):
                piece = tile if kj == 1 else shifted(wide, lane96, kj - 1).astype(BF)
                for ki in range(3):
                    i = r - ki
                    if 0 <= i < HR:
                        base = (ki * 3 + kj) * C
                        q_ref[base : base + C, g * FW + i * W : g * FW + (i + 1) * W] = piece

    srow = lax.broadcasted_iota(jnp.int32, (C, GROWS), 0)
    scol = lax.broadcasted_iota(jnp.int32, (C, GROWS), 1)
    pick = ((srow // 32 == scol % OPAD) & (srow % 32 == scol // OPAD)).astype(F32).astype(BF)
    wo = wo_ref[...]
    wo8 = tn(pick, wo).astype(BF)
    wo8t = tn(wo, pick).astype(BF)

    col = lax.broadcasted_iota(jnp.int32, (1, FW), 1)
    outside = ((col < W) & first) | ((col >= 3 * W) & last)
    keep = jnp.where(outside, 0.0, 1.0)
    def conv(f):
        low = max(0, f - 2) * C
        r_ref[f, low:, :] = nn(wt_ref[low:, :], q_ref[:KT, f * FW : (f + 1) * FW])

    def activate(f):
        pre = cb_ref[...]
        for kt in range(2, max(-1, 1 - f), -1):
            pre = pre + r_ref[f + kt - 2, kt * C : (kt + 1) * C, :]
        sig = jax.nn.sigmoid(pre)
        hid_ref[:, f * FW : (f + 1) * FW] = (pre * sig * keep).astype(BF)
        fac_ref[:, f * FW : (f + 1) * FW] = sig * (1.0 + pre * (1.0 - sig)) * keep

    def project(f):
        y_ref[:, f * FW : (f + 1) * FW] = nn(wo8, hid_ref[:, f * FW : (f + 1) * FW])

    for f in range(F + 2):
        if f < F:
            conv(f)
        if 1 <= f <= F:
            activate(f - 1)
        if f >= 2:
            project(f - 2)

    grads = {}
    obsum = jnp.zeros((OPAD, W), F32)
    for f in range(F):
        decs = []
        for i in range(2):
            dec = None
            for kj in range(3):
                z = None
                for kt in range(3):
                    g = f + kt - 2
                    if g < 0:
                        continue
                    for ki in range(3):
                        t = kt * 9 + ki * 3 + kj
                        at = g * FW + (i + ki) * W
                        v = y_ref[t * OPAD : (t + 1) * OPAD, at : at + W]
                        z = v if z is None else z + v
                z = shifted(z, lane8, kj - 1)
                dec = z if dec is None else dec + z
            dec = (dec + ob_ref[...]).astype(BF)
            at = (f * 2 + i) * W
            decs.append(dec.astype(F32))
            gf = ((dec.astype(F32) - tgt_ref[:, at : at + W]) * scale).astype(BF).astype(F32)
            obsum = obsum + gf
            for kj in range(3):
                grads[f, i, kj] = shifted(gf, lane8, 1 - kj)
        for o in range(3):
            rows = jnp.concatenate([d[o : o + 1] for d in decs], axis=0)
            dec_ref[0, o, f] = rows.astype(BF)

    none = jnp.zeros((OPAD, W), F32)
    for g in range(F):
        for i in range(HR):
            parts = []
            for t in range(TPAD):
                kt, ki, kj = t // 9, t // 3 % 3, t % 3
                parts.append(grads.get((g + 2 - kt, i - ki, kj), none) if t < TAPS else none)
            at = g * FW + i * W
            for p in range(TPAD // 2):
                both = jnp.concatenate(parts[2 * p : 2 * p + 2], axis=0).astype(BF)
                g_ref[p * 16 : (p + 1) * 16, at : at + W] = both

    gh_ref[C:W, :] = jnp.zeros((W - C, POS), BF)
    gh_ref[W + C :, :] = jnp.zeros((W - C, POS), BF)
    gh_ref[W:, POS - FW :] = jnp.zeros((W, FW), BF)
    for f in range(F):
        back = nn(wo8t, g_ref[:, f * FW : (f + 1) * FW])
        gh = (back * fac_ref[:, f * FW : (f + 1) * FW]).astype(BF)
        gh_ref[:C, f * FW : (f + 1) * FW] = gh
        if f:
            gh_ref[W : W + C, (f - 1) * FW : f * FW] = gh

    both = nt(q_ref[...], gh_ref[...])
    main_ref[2 * KT : NW, :] = both[:KT, :W]
    main_ref[NW:, :] = both[KT:, :W]
    main_ref[KT : 2 * KT, :] = both[:KT, W:]
    main_ref[:KT, :] = nt(q_ref[:KT, : 3 * FW], gh_ref[:W, 2 * FW :])
    gow = nt(g_ref[...], hid_ref[...]).astype(BF)
    gow = nn(pick, gow)
    bias = main_ref[NW : NW + OPAD, :]
    obias = jnp.broadcast_to(jnp.sum(obsum, axis=1, keepdims=True), (OPAD, W))

    lane = lax.broadcasted_iota(jnp.int32, (TAIL, W), 1)
    for k in range(3):
        lo, hi = k * TAIL, (k + 1) * TAIL
        tail = pltpu.roll(main_ref[MAIN:NW, :], 96 - 32 * k, 1)
        if hi <= MAIN:
            head = main_ref[lo:hi, :]
        else:
            head = jnp.concatenate(
                [main_ref[lo:MAIN, :], jnp.pad(gow, ((0, 0), (0, W - C)))], axis=0
            )
        out_ref[lo:hi, :] = jnp.where(lane < C, head, tail).astype(BF)
    ends = []
    for v in (bias, obias):
        top = v.astype(BF).astype(F32)
        ends += [top, v - top]
    out_ref[ROWS - 32 :, :] = jnp.concatenate(ends, axis=0).astype(BF)


def split_sums(total, is_last):
    out = total.astype(BF)
    start = total.shape[0] - 32
    fixed = []
    for at in (start, start + 16):
        whole = total[at : at + 8] + total[at + 8 : at + 16]
        top = whole.astype(BF).astype(F32)
        fixed += [top, whole - top]
    special = jnp.concatenate(([total[:start]] if start else []) + fixed, axis=0).astype(BF)
    return jnp.where(is_last, special, out)


def in_last():
    last = math.prod(lax.axis_size(a) for a in NEAR) - 1
    return flat_index(NEAR) == last ^ FIRST


def pass_on(value, pairs):
    outer, inner = (lax.axis_size(a) for a in DEPTH)
    place = [(d % inner) * outer + d // inner for d in range(outer * inner)]
    return lax.ppermute(value, DEPTH[::-1], [(place[i], place[j]) for i, j in pairs])


def plane_sum_kernel(in_ref, out_ref):
    total = in_ref[0].astype(F32)
    for k in range(1, in_ref.shape[0]):
        total = total + in_ref[k].astype(F32)
    out_ref[...] = split_sums(total, in_last())


def depth_sum_kernel(*refs):
    *in_refs, out_ref = refs
    total = in_refs[0][...].astype(F32)
    for ref in in_refs[1:]:
        total = total + ref[...].astype(F32)
    out_ref[...] = jnp.where(flat_index(DEPTH) < 2, split_sums(total, in_last()), jnp.zeros_like(out_ref))


def side_sum_kernel(part_ref, side_ref, out_ref):
    total = part_ref[...].astype(F32) + side_ref[...].astype(F32)
    at = flat_index(DEPTH)
    out_ref[...] = jnp.where((at == 2) | (at == 6), split_sums(total, in_last()), part_ref[...])


def copies_kernel(one_ref, two_ref, out_ref):
    either = one_ref[...] + two_ref[...]
    for k in range(out_ref.shape[0]):
        out_ref[k] = either


def unpack_kernel(in_ref, gw_ref, gb_ref, go_ref, gob_ref):
    def get(lo, hi):
        return in_ref[lo:hi, :].astype(F32)

    gw_ref[:MAIN, :] = get(0, MAIN)[:, :C]
    lane = lax.broadcasted_iota(jnp.int32, (TAIL, W), 1)
    tail = None
    for k in range(3):
        v = pltpu.roll(get(k * TAIL, (k + 1) * TAIL), 32 + 32 * k, 1)
        tail = v if tail is None else jnp.where(lane < 32 * k, tail, v)
    gw_ref[MAIN:, :] = tail[:, :C]
    gow = get(MAIN, MAIN + 96)
    for o in range(3):
        go_ref[o] = gow[o * 32 : o * 32 + TAPS, :C]
    sums = get(2016, 2048)
    gb_ref[...] = (sums[0:8] + sums[8:16])[0, :C]
    ob = sums[16:24] + sums[24:32]
    r8 = lax.broadcasted_iota(jnp.int32, (OPAD, W), 0)
    l8 = lax.broadcasted_iota(jnp.int32, (OPAD, W), 1)
    gob_ref[...] = jnp.sum(jnp.where(r8 == l8, ob, 0.0), axis=0)[:3]


VM = functools.partial(pl.BlockSpec, memory_space=pltpu.VMEM)
LIMIT = 48 * 1024 * 1024
SMALL = 4 * 1024 * 1024


def k1_call(n_rows, scale):
    return pl.pallas_call(
        functools.partial(device_kernel, n_rows, scale),
        out_shape=(
            jax.ShapeDtypeStruct((1, 3, F, 2, W), BF),
            jax.ShapeDtypeStruct((ROWS, W), BF),
        ),
        in_specs=[VM()] * 8,
        out_specs=(VM(), VM()),
        scratch_shapes=[
            pltpu.VMEM((KT + 16, POS), BF),
            pltpu.VMEM((F, 3 * C, FW), F32),
            pltpu.VMEM((C, POS), BF),
            pltpu.VMEM((C, POS), F32),
            pltpu.VMEM((GROWS, POS), F32),
            pltpu.VMEM((GROWS, POS), BF),
            pltpu.VMEM((2 * W, POS), BF),
            pltpu.VMEM((NW + 16, W), F32),
        ],
        compiler_params=pltpu.CompilerParams(vmem_limit_bytes=LIMIT),
        name="device_part",
    )


def local(latent_features, conv_weight, conv_bias, out_weight, out_bias, target_frames):
    sizes = [lax.axis_size(a) for a in EDGE_AXES]
    n_rows = math.prod(sizes)
    near = math.prod(lax.axis_size(a) for a in NEAR)
    clips = lax.axis_size("zh") * lax.axis_size("c")
    scale = 1.0 / math.sqrt(3 * clips * F * 2 * n_rows * W)

    own = jnp.transpose(latent_features[0], (1, 2, 0, 3))
    even = [(i, i ^ 1) for i in range(n_rows)]
    odd = [(i, ((i + 1) ^ 1) - 1) for i in range(1, n_rows - 1)]
    axes = EDGE_AXES + ("c",)
    one = lax.ppermute(own, axes, [(2 * i, 2 * j) for i, j in even] + [(2 * i + 1, 2 * j + 1) for i, j in odd])
    two = lax.ppermute(own, axes, [(2 * i, 2 * j) for i, j in odd] + [(2 * i + 1, 2 * j + 1) for i, j in even])

    wt = jnp.transpose(conv_weight.reshape(3, KT, C), (0, 2, 1)).reshape(3 * C, KT)
    wo = jnp.pad(jnp.transpose(out_weight, (2, 0, 1)), ((0, 0), (0, 5), (0, 0))).reshape(C, C)
    ob = jnp.pad(out_bias[:, None], ((0, 5), (0, 0)))
    tgt = jnp.pad(target_frames[0].reshape(3, F * 2 * W).astype(F32), ((0, 5), (0, 0)))

    decoded, packed = k1_call(n_rows, scale)(own, one, two, wt, conv_bias[:, None], wo, ob, tgt)

    chunk = ROWS // near

    def small(kernel, name, copies, *operands):
        return pl.pallas_call(
            kernel,
            out_shape=jax.ShapeDtypeStruct(copies + (chunk, W), BF),
            in_specs=[VM()] * len(operands),
            out_specs=VM(),
            compiler_params=pltpu.CompilerParams(vmem_limit_bytes=SMALL),
            name=name,
        )(*operands)

    parts = lax.all_to_all(packed.reshape(near, chunk, W), AXES, 0, 0, axis_index_groups=scatter_groups())
    part = small(plane_sum_kernel, "plane_sum", (), parts)
    side = pass_on(part, SIDE)
    more = small(side_sum_kernel, "side_sum", (), part, side)
    close = [pass_on(more, pairs) for pairs in CLOSE[::-1]]
    far = [pass_on(part, pairs) for pairs in FAR[::-1]]
    total = small(depth_sum_kernel, "depth_sum", (), part, *close, *far)
    received = [pass_on(total, pairs) for pairs in SPREAD[:-1]]
    total = sum(received, total)
    outer = pass_on(total, SPREAD[-1])
    parts = small(copies_kernel, "copies", (near,), total, outer)
    parts = lax.all_to_all(parts, AXES, 0, 0, axis_index_groups=scatter_groups())

    gw, gb, go, gob = pl.pallas_call(
        unpack_kernel,
        out_shape=(
            jax.ShapeDtypeStruct((NW, C), F32),
            jax.ShapeDtypeStruct((C,), F32),
            jax.ShapeDtypeStruct((3, TAPS, C), F32),
            jax.ShapeDtypeStruct((3,), F32),
        ),
        in_specs=[VM()],
        out_specs=(VM(),) * 4,
        compiler_params=pltpu.CompilerParams(vmem_limit_bytes=2 * SMALL),
        name="unpack",
    )(parts.reshape(ROWS, W))
    return (
        decoded,
        gw.reshape(TAPS, C, C),
        gb,
        jnp.transpose(go, (1, 2, 0)),
        gob,
    )


def solution(mesh):
    split = Mesh(mesh.devices.reshape(4, 2, 2, 4, 4, 2), AXES)
    frames = P(("zh", "c"), None, None, EDGE_AXES, None)
    return jax.shard_map(
        local,
        mesh=split,
        in_specs=(frames, P(), P(), P(), P(), frames),
        out_specs=(frames, P(), P(), P(), P()),
        check_vma=False,
    )
```

```python
import functools
import math

import jax
import jax.numpy as jnp
from jax import lax
from jax.experimental import pallas as pl
from jax.experimental.pallas import tpu as pltpu
from jax.sharding import Mesh, PartitionSpec as P

BF = jnp.bfloat16
F32 = jnp.float32
C = 96
F = 5
W = 128
TAPS = 27
TPAD = 28
OPAD = 8
GROWS = TPAD * OPAD
HR = 4
FW = HR * W
POS = F * FW
KT = 9 * C
NW = TAPS * C
MAIN = 1920
TAIL = NW - MAIN
ROWS = 2048
AXES = ("x", "z1", "z0", "y", "zh", "c")
EDGE_AXES = ("x", "z1", "z0", "y")
NEAR = ("x", "z0", "y", "c")
DEPTH = ("zh", "z1")
FAR = (((5, 0), (4, 1)), ((4, 0), (5, 1)))
SIDE = ((7, 6), (3, 2))
CLOSE = (((6, 1), (2, 0)), ((6, 0), (2, 1)), ((1, 0), (0, 1)))
SPREAD = (((1, 7),), ((0, 2), (1, 3)), ((2, 4), (3, 5), (7, 6)))


def nt(a, b):
    return lax.dot_general(a, b, (((1,), (1,)), ((), ())), preferred_element_type=F32)


def nn(a, b):
    return lax.dot_general(a, b, (((1,), (0,)), ((), ())), preferred_element_type=F32)


def tn(a, b):
    return lax.dot_general(a, b, (((0,), (0,)), ((), ())), preferred_element_type=F32)


def shifted(v, lane, by):
    if by == 0:
        return v
    if by > 0:
        return jnp.where(lane < W - 1, pltpu.roll(v, W - 1, 1), 0.0)
    return jnp.where(lane > 0, pltpu.roll(v, 1, 1), 0.0)


FIRST = 41


def scatter_groups():
    nx, nz1, nz0, ny, nzh, nc = (lax.axis_size(a) for a in AXES)
    groups = []
    for z1 in range(nz1):
        for zh in range(nzh):
            members = []
            for place in range(nx * nz0 * ny * nc):
                rest, c = divmod(place ^ FIRST, nc)
                rest, y = divmod(rest, ny)
                x, z0 = divmod(rest, nz0)
                members.append(((((x * nz1 + z1) * nz0 + z0) * ny + y) * nzh + zh) * nc + c)
            groups.append(members)
    return groups


def flat_index(axes):
    index = 0
    for axis in axes:
        index = index * lax.axis_size(axis) + lax.axis_index(axis)
    return index


def device_kernel(
    n_rows, scale,
    own_ref, one_ref, two_ref, wt_ref, cb_ref, wo_ref, ob_ref, tgt_ref,
    dec_ref, out_ref,
    q_ref, r_ref, hid_ref, fac_ref, y_ref, g_ref, gh_ref, main_ref,
):
    row_id = flat_index(EDGE_AXES)
    prev_first = lax.rem(row_id + lax.axis_index("c"), 2) == 1
    first = row_id == 0
    last = row_id == n_rows - 1
    lane96 = lax.broadcasted_iota(jnp.int32, (C, W), 1)
    lane8 = lax.broadcasted_iota(jnp.int32, (OPAD, W), 1)

    q_ref[KT:, :] = jnp.ones((16, POS), BF)
    for g in range(F):
        for r in range(6):
            if r < 2:
                tile = jnp.where(prev_first, one_ref[g, r], two_ref[g, r])
            elif r < 4:
                tile = own_ref[g, r - 2]
            else:
                tile = jnp.where(prev_first, two_ref[g, r - 4], one_ref[g, r - 4])
            wide = tile.astype(F32)
            for kj in range(3):
                piece = tile if kj == 1 else shifted(wide, lane96, kj - 1).astype(BF)
                for ki in range(3):
                    i = r - ki
                    if 0 <= i < HR:
                        base = (ki * 3 + kj) * C
                        q_ref[base : base + C, g * FW + i * W : g * FW + (i + 1) * W] = piece

    srow = lax.broadcasted_iota(jnp.int32, (C, GROWS), 0)
    scol = lax.broadcasted_iota(jnp.int32, (C, GROWS), 1)
    pick = ((srow // 32 == scol % OPAD) & (srow % 32 == scol // OPAD)).astype(F32).astype(BF)
    wo = wo_ref[...]
    wo8 = tn(pick, wo).astype(BF)
    wo8t = tn(wo, pick).astype(BF)

    col = lax.broadcasted_iota(jnp.int32, (1, FW), 1)
    outside = ((col < W) & first) | ((col >= 3 * W) & last)
    keep = jnp.where(outside, 0.0, 1.0)
    def conv(f):
        low = max(0, f - 2) * C
        r_ref[f, low:, :] = nn(wt_ref[low:, :], q_ref[:KT, f * FW : (f + 1) * FW])

    def activate(f):
        pre = cb_ref[...]
        for kt in range(2, max(-1, 1 - f), -1):
            pre = pre + r_ref[f + kt - 2, kt * C : (kt + 1) * C, :]
        sig = jax.nn.sigmoid(pre)
        hid_ref[:, f * FW : (f + 1) * FW] = (pre * sig * keep).astype(BF)
        fac_ref[:, f * FW : (f + 1) * FW] = sig * (1.0 + pre * (1.0 - sig)) * keep

    def project(f):
        y_ref[:, f * FW : (f + 1) * FW] = nn(wo8, hid_ref[:, f * FW : (f + 1) * FW])

    for f in range(F + 2):
        if f < F:
            conv(f)
        if 1 <= f <= F:
            activate(f - 1)
        if f >= 2:
            project(f - 2)

    grads = {}
    obsum = jnp.zeros((OPAD, W), F32)
    for f in range(F):
        decs = []
        for i in range(2):
            dec = None
            for kj in range(3):
                z = None
                for kt in range(3):
                    g = f + kt - 2
                    if g < 0:
                        continue
                    for ki in range(3):
                        t = kt * 9 + ki * 3 + kj
                        at = g * FW + (i + ki) * W
                        v = y_ref[t * OPAD : (t + 1) * OPAD, at : at + W]
                        z = v if z is None else z + v
                z = shifted(z, lane8, kj - 1)
                dec = z if dec is None else dec + z
            dec = (dec + ob_ref[...]).astype(BF)
            at = (f * 2 + i) * W
            decs.append(dec.astype(F32))
            gf = ((dec.astype(F32) - tgt_ref[:, at : at + W]) * scale).astype(BF).astype(F32)
            obsum = obsum + gf
            for kj in range(3):
                grads[f, i, kj] = shifted(gf, lane8, 1 - kj)
        for o in range(3):
            rows = jnp.concatenate([d[o : o + 1] for d in decs], axis=0)
            dec_ref[0, o, f] = rows.astype(BF)

    none = jnp.zeros((OPAD, W), F32)
    for g in range(F):
        for i in range(HR):
            parts = []
            for t in range(TPAD):
                kt, ki, kj = t // 9, t // 3 % 3, t % 3
                parts.append(grads.get((g + 2 - kt, i - ki, kj), none) if t < TAPS else none)
            at = g * FW + i * W
            for p in range(TPAD // 2):
                both = jnp.concatenate(parts[2 * p : 2 * p + 2], axis=0).astype(BF)
                g_ref[p * 16 : (p + 1) * 16, at : at + W] = both

    gh_ref[C:W, :] = jnp.zeros((W - C, POS), BF)
    gh_ref[W + C :, :] = jnp.zeros((W - C, POS), BF)
    gh_ref[W:, POS - FW :] = jnp.zeros((W, FW), BF)
    for f in range(F):
        back = nn(wo8t, g_ref[:, f * FW : (f + 1) * FW])
        gh = (back * fac_ref[:, f * FW : (f + 1) * FW]).astype(BF)
        gh_ref[:C, f * FW : (f + 1) * FW] = gh
        if f:
            gh_ref[W : W + C, (f - 1) * FW : f * FW] = gh

    both = nt(q_ref[...], gh_ref[...])
    main_ref[2 * KT : NW, :] = both[:KT, :W]
    main_ref[NW:, :] = both[KT:, :W]
    main_ref[KT : 2 * KT, :] = both[:KT, W:]
    main_ref[:KT, :] = nt(q_ref[:KT, : 3 * FW], gh_ref[:W, 2 * FW :])
    gow = nt(g_ref[...], hid_ref[...]).astype(BF)
    gow = nn(pick, gow)
    bias = main_ref[NW : NW + OPAD, :]
    obias = jnp.broadcast_to(jnp.sum(obsum, axis=1, keepdims=True), (OPAD, W))

    lane = lax.broadcasted_iota(jnp.int32, (TAIL, W), 1)
    for k in range(3):
        lo, hi = k * TAIL, (k + 1) * TAIL
        tail = pltpu.roll(main_ref[MAIN:NW, :], 96 - 32 * k, 1)
        if hi <= MAIN:
            head = main_ref[lo:hi, :]
        else:
            head = jnp.concatenate(
                [main_ref[lo:MAIN, :], jnp.pad(gow, ((0, 0), (0, W - C)))], axis=0
            )
        out_ref[lo:hi, :] = jnp.where(lane < C, head, tail).astype(BF)
    ends = []
    for v in (bias, obias):
        top = v.astype(BF).astype(F32)
        ends += [top, v - top]
    out_ref[ROWS - 32 :, :] = jnp.concatenate(ends, axis=0).astype(BF)


def split_sums(total, is_last):
    out = total.astype(BF)
    start = total.shape[0] - 32
    fixed = []
    for at in (start, start + 16):
        whole = total[at : at + 8] + total[at + 8 : at + 16]
        top = whole.astype(BF).astype(F32)
        fixed += [top, whole - top]
    special = jnp.concatenate(([total[:start]] if start else []) + fixed, axis=0).astype(BF)
    return jnp.where(is_last, special, out)


def in_last():
    last = math.prod(lax.axis_size(a) for a in NEAR) - 1
    return flat_index(NEAR) == last ^ FIRST


def pass_on(value, pairs):
    outer, inner = (lax.axis_size(a) for a in DEPTH)
    place = [(d % inner) * outer + d // inner for d in range(outer * inner)]
    return lax.ppermute(value, DEPTH[::-1], [(place[i], place[j]) for i, j in pairs])


def plane_sum_kernel(in_ref, out_ref):
    total = in_ref[0].astype(F32)
    for k in range(1, in_ref.shape[0]):
        total = total + in_ref[k].astype(F32)
    out_ref[...] = split_sums(total, in_last())


def depth_sum_kernel(*refs):
    *in_refs, out_ref = refs
    total = in_refs[0][...].astype(F32)
    for ref in in_refs[1:]:
        total = total + ref[...].astype(F32)
    out_ref[...] = jnp.where(flat_index(DEPTH) < 2, split_sums(total, in_last()), jnp.zeros_like(out_ref))


def side_sum_kernel(part_ref, side_ref, out_ref):
    total = part_ref[...].astype(F32) + side_ref[...].astype(F32)
    at = flat_index(DEPTH)
    out_ref[...] = jnp.where((at == 2) | (at == 6), split_sums(total, in_last()), part_ref[...])


def copies_kernel(one_ref, two_ref, out_ref):
    either = one_ref[...] + two_ref[...]
    for k in range(out_ref.shape[0]):
        out_ref[k] = either


def unpack_kernel(in_ref, gw_ref, gb_ref, go_ref, gob_ref):
    def get(lo, hi):
        return in_ref[lo:hi, :].astype(F32)

    gw_ref[:MAIN, :] = get(0, MAIN)[:, :C]
    lane = lax.broadcasted_iota(jnp.int32, (TAIL, W), 1)
    tail = None
    for k in range(3):
        v = pltpu.roll(get(k * TAIL, (k + 1) * TAIL), 32 + 32 * k, 1)
        tail = v if tail is None else jnp.where(lane < 32 * k, tail, v)
    gw_ref[MAIN:, :] = tail[:, :C]
    gow = get(MAIN, MAIN + 96)
    for o in range(3):
        go_ref[o] = gow[o * 32 : o * 32 + TAPS, :C]
    sums = get(2016, 2048)
    gb_ref[...] = (sums[0:8] + sums[8:16])[0, :C]
    ob = sums[16:24] + sums[24:32]
    r8 = lax.broadcasted_iota(jnp.int32, (OPAD, W), 0)
    l8 = lax.broadcasted_iota(jnp.int32, (OPAD, W), 1)
    gob_ref[...] = jnp.sum(jnp.where(r8 == l8, ob, 0.0), axis=0)[:3]


VM = functools.partial(pl.BlockSpec, memory_space=pltpu.VMEM)
LIMIT = 48 * 1024 * 1024
SMALL = 4 * 1024 * 1024


def k1_call(n_rows, scale):
    return pl.pallas_call(
        functools.partial(device_kernel, n_rows, scale),
        out_shape=(
            jax.ShapeDtypeStruct((1, 3, F, 2, W), BF),
            jax.ShapeDtypeStruct((ROWS, W), BF),
        ),
        in_specs=[VM()] * 8,
        out_specs=(VM(), VM()),
        scratch_shapes=[
            pltpu.VMEM((KT + 16, POS), BF),
            pltpu.VMEM((F, 3 * C, FW), F32),
            pltpu.VMEM((C, POS), BF),
            pltpu.VMEM((C, POS), F32),
            pltpu.VMEM((GROWS, POS), F32),
            pltpu.VMEM((GROWS, POS), BF),
            pltpu.VMEM((2 * W, POS), BF),
            pltpu.VMEM((NW + 16, W), F32),
        ],
        compiler_params=pltpu.CompilerParams(vmem_limit_bytes=LIMIT),
        name="device_part",
    )


def local(latent_features, conv_weight, conv_bias, out_weight, out_bias, target_frames):
    sizes = [lax.axis_size(a) for a in EDGE_AXES]
    n_rows = math.prod(sizes)
    near = math.prod(lax.axis_size(a) for a in NEAR)
    clips = lax.axis_size("zh") * lax.axis_size("c")
    scale = 1.0 / math.sqrt(3 * clips * F * 2 * n_rows * W)

    own = jnp.transpose(latent_features[0], (1, 2, 0, 3))
    even = [(i, i ^ 1) for i in range(n_rows)]
    odd = [(i, ((i + 1) ^ 1) - 1) for i in range(1, n_rows - 1)]
    axes = EDGE_AXES + ("c",)
    one = lax.ppermute(own, axes, [(2 * i, 2 * j) for i, j in even] + [(2 * i + 1, 2 * j + 1) for i, j in odd])
    two = lax.ppermute(own, axes, [(2 * i, 2 * j) for i, j in odd] + [(2 * i + 1, 2 * j + 1) for i, j in even])

    wt = jnp.transpose(conv_weight.reshape(3, KT, C), (0, 2, 1)).reshape(3 * C, KT)
    wo = jnp.pad(jnp.transpose(out_weight, (2, 0, 1)), ((0, 0), (0, 5), (0, 0))).reshape(C, C)
    ob = jnp.pad(out_bias[:, None], ((0, 5), (0, 0)))
    tgt = jnp.pad(target_frames[0].reshape(3, F * 2 * W).astype(F32), ((0, 5), (0, 0)))

    decoded, packed = k1_call(n_rows, scale)(own, one, two, wt, conv_bias[:, None], wo, ob, tgt)

    chunk = ROWS // near

    def small(kernel, name, copies, *operands):
        return pl.pallas_call(
            kernel,
            out_shape=jax.ShapeDtypeStruct(copies + (chunk, W), BF),
            in_specs=[VM()] * len(operands),
            out_specs=VM(),
            compiler_params=pltpu.CompilerParams(vmem_limit_bytes=SMALL),
            name=name,
        )(*operands)

    parts = lax.all_to_all(packed.reshape(near, chunk, W), AXES, 0, 0, axis_index_groups=scatter_groups())
    part = small(plane_sum_kernel, "plane_sum", (), parts)
    side = pass_on(part, SIDE)
    more = small(side_sum_kernel, "side_sum", (), part, side)
    close = [pass_on(more, pairs) for pairs in CLOSE[::-1]]
    far = [pass_on(part, pairs) for pairs in FAR[::-1]]
    total = small(depth_sum_kernel, "depth_sum", (), part, *close, *far)
    received = [pass_on(total, pairs) for pairs in SPREAD[:-1]]
    total = sum(received, total)
    outer = pass_on(total, SPREAD[-1])
    parts = small(copies_kernel, "copies", (near,), total, outer)
    parts = lax.all_to_all(parts, AXES, 0, 0, axis_index_groups=scatter_groups())

    gw, gb, go, gob = pl.pallas_call(
        unpack_kernel,
        out_shape=(
            jax.ShapeDtypeStruct((NW, C), F32),
            jax.ShapeDtypeStruct((C,), F32),
            jax.ShapeDtypeStruct((3, TAPS, C), F32),
            jax.ShapeDtypeStruct((3,), F32),
        ),
        in_specs=[VM()],
        out_specs=(VM(),) * 4,
        compiler_params=pltpu.CompilerParams(vmem_limit_bytes=2 * SMALL),
        name="unpack",
    )(parts.reshape(ROWS, W))
    return (
        decoded,
        gw.reshape(TAPS, C, C),
        gb,
        jnp.transpose(go, (1, 2, 0)),
        gob,
    )


def solution(mesh):
    split = Mesh(mesh.devices.reshape(4, 2, 2, 4, 4, 2), AXES)
    frames = P(("zh", "c"), None, None, EDGE_AXES, None)
    return jax.shard_map(
        local,
        mesh=split,
        in_specs=(frames, P(), P(), P(), P(), frames),
        out_specs=(frames, P(), P(), P(), P()),
        check_vma=False,
    )
```

```python
import functools
import math

import jax
import jax.numpy as jnp
from jax import lax
from jax.experimental import pallas as pl
from jax.experimental.pallas import tpu as pltpu
from jax.sharding import Mesh, PartitionSpec as P

BF = jnp.bfloat16
F32 = jnp.float32
C = 96
F = 5
W = 128
TAPS = 27
TPAD = 28
OPAD = 8
GROWS = TPAD * OPAD
HR = 4
FW = HR * W
POS = F * FW
KT = 9 * C
NW = TAPS * C
MAIN = 1920
TAIL = NW - MAIN
ROWS = 2048
AXES = ("x", "z1", "z0", "y", "zh", "c")
EDGE_AXES = ("x", "z1", "z0", "y")
NEAR = ("x", "z0", "y", "c")
DEPTH = ("zh", "z1")
FAR = (((4, 0), (5, 1)), ((5, 0), (4, 1)))
SIDE = ((7, 6), (3, 2))
CLOSE = (((6, 1), (2, 0)), ((6, 0), (2, 1)), ((1, 0), (0, 1)))
SPREAD = (((1, 7),), ((0, 2), (1, 3)), ((2, 4), (3, 5), (7, 6)))


def nt(a, b):
    return lax.dot_general(a, b, (((1,), (1,)), ((), ())), preferred_element_type=F32)


def nn(a, b):
    return lax.dot_general(a, b, (((1,), (0,)), ((), ())), preferred_element_type=F32)


def tn(a, b):
    return lax.dot_general(a, b, (((0,), (0,)), ((), ())), preferred_element_type=F32)


def shifted(v, lane, by):
    if by == 0:
        return v
    if by > 0:
        return jnp.where(lane < W - 1, pltpu.roll(v, W - 1, 1), 0.0)
    return jnp.where(lane > 0, pltpu.roll(v, 1, 1), 0.0)


FIRST = 43


def scatter_groups():
    nx, nz1, nz0, ny, nzh, nc = (lax.axis_size(a) for a in AXES)
    groups = []
    for z1 in range(nz1):
        for zh in range(nzh):
            members = []
            for place in range(nx * nz0 * ny * nc):
                rest, c = divmod(place ^ FIRST, nc)
                rest, y = divmod(rest, ny)
                x, z0 = divmod(rest, nz0)
                members.append(((((x * nz1 + z1) * nz0 + z0) * ny + y) * nzh + zh) * nc + c)
            groups.append(members)
    return groups


def flat_index(axes):
    index = 0
    for axis in axes:
        index = index * lax.axis_size(axis) + lax.axis_index(axis)
    return index


def device_kernel(
    n_rows, scale,
    own_ref, one_ref, two_ref, wt_ref, cb_ref, wo_ref, ob_ref, tgt_ref,
    dec_ref, out_ref,
    q_ref, r_ref, hid_ref, fac_ref, y_ref, g_ref, gh_ref, main_ref,
):
    row_id = flat_index(EDGE_AXES)
    prev_first = lax.rem(row_id + lax.axis_index("c"), 2) == 1
    first = row_id == 0
    last = row_id == n_rows - 1
    lane96 = lax.broadcasted_iota(jnp.int32, (C, W), 1)
    lane8 = lax.broadcasted_iota(jnp.int32, (OPAD, W), 1)

    q_ref[KT:, :] = jnp.ones((16, POS), BF)
    for g in range(F):
        for r in range(6):
            if r < 2:
                tile = jnp.where(prev_first, one_ref[g, r], two_ref[g, r])
            elif r < 4:
                tile = own_ref[g, r - 2]
            else:
                tile = jnp.where(prev_first, two_ref[g, r - 4], one_ref[g, r - 4])
            wide = tile.astype(F32)
            for kj in range(3):
                piece = tile if kj == 1 else shifted(wide, lane96, kj - 1).astype(BF)
                for ki in range(3):
                    i = r - ki
                    if 0 <= i < HR:
                        base = (ki * 3 + kj) * C
                        q_ref[base : base + C, g * FW + i * W : g * FW + (i + 1) * W] = piece

    srow = lax.broadcasted_iota(jnp.int32, (C, GROWS), 0)
    scol = lax.broadcasted_iota(jnp.int32, (C, GROWS), 1)
    pick = ((srow // 32 == scol % OPAD) & (srow % 32 == scol // OPAD)).astype(F32).astype(BF)
    wo = wo_ref[...]
    wo8 = tn(pick, wo).astype(BF)
    wo8t = tn(wo, pick).astype(BF)

    col = lax.broadcasted_iota(jnp.int32, (1, FW), 1)
    outside = ((col < W) & first) | ((col >= 3 * W) & last)
    keep = jnp.where(outside, 0.0, 1.0)
    def conv(f):
        low = max(0, f - 2) * C
        r_ref[f, low:, :] = nn(wt_ref[low:, :], q_ref[:KT, f * FW : (f + 1) * FW])

    def activate(f):
        pre = cb_ref[...]
        for kt in range(2, max(-1, 1 - f), -1):
            pre = pre + r_ref[f + kt - 2, kt * C : (kt + 1) * C, :]
        sig = jax.nn.sigmoid(pre)
        hid_ref[:, f * FW : (f + 1) * FW] = (pre * sig * keep).astype(BF)
        fac_ref[:, f * FW : (f + 1) * FW] = sig * (1.0 + pre * (1.0 - sig)) * keep

    def project(f):
        y_ref[:, f * FW : (f + 1) * FW] = nn(wo8, hid_ref[:, f * FW : (f + 1) * FW])

    for f in range(F + 2):
        if f < F:
            conv(f)
        if 1 <= f <= F:
            activate(f - 1)
        if f >= 2:
            project(f - 2)

    grads = {}
    obsum = jnp.zeros((OPAD, W), F32)
    for f in range(F):
        decs = []
        for i in range(2):
            dec = None
            for kj in range(3):
                z = None
                for kt in range(3):
                    g = f + kt - 2
                    if g < 0:
                        continue
                    for ki in range(3):
                        t = kt * 9 + ki * 3 + kj
                        at = g * FW + (i + ki) * W
                        v = y_ref[t * OPAD : (t + 1) * OPAD, at : at + W]
                        z = v if z is None else z + v
                z = shifted(z, lane8, kj - 1)
                dec = z if dec is None else dec + z
            dec = (dec + ob_ref[...]).astype(BF)
            at = (f * 2 + i) * W
            decs.append(dec.astype(F32))
            gf = ((dec.astype(F32) - tgt_ref[:, at : at + W]) * scale).astype(BF).astype(F32)
            obsum = obsum + gf
            for kj in range(3):
                grads[f, i, kj] = shifted(gf, lane8, 1 - kj)
        for o in range(3):
            rows = jnp.concatenate([d[o : o + 1] for d in decs], axis=0)
            dec_ref[0, o, f] = rows.astype(BF)

    none = jnp.zeros((OPAD, W), F32)
    for g in range(F):
        for i in range(HR):
            parts = []
            for t in range(TPAD):
                kt, ki, kj = t // 9, t // 3 % 3, t % 3
                parts.append(grads.get((g + 2 - kt, i - ki, kj), none) if t < TAPS else none)
            at = g * FW + i * W
            for p in range(TPAD // 2):
                both = jnp.concatenate(parts[2 * p : 2 * p + 2], axis=0).astype(BF)
                g_ref[p * 16 : (p + 1) * 16, at : at + W] = both

    gh_ref[C:W, :] = jnp.zeros((W - C, POS), BF)
    gh_ref[W + C :, :] = jnp.zeros((W - C, POS), BF)
    gh_ref[W:, POS - FW :] = jnp.zeros((W, FW), BF)
    for f in range(F):
        back = nn(wo8t, g_ref[:, f * FW : (f + 1) * FW])
        gh = (back * fac_ref[:, f * FW : (f + 1) * FW]).astype(BF)
        gh_ref[:C, f * FW : (f + 1) * FW] = gh
        if f:
            gh_ref[W : W + C, (f - 1) * FW : f * FW] = gh

    both = nt(q_ref[...], gh_ref[...])
    main_ref[2 * KT : NW, :] = both[:KT, :W]
    main_ref[NW:, :] = both[KT:, :W]
    main_ref[KT : 2 * KT, :] = both[:KT, W:]
    main_ref[:KT, :] = nt(q_ref[:KT, : 3 * FW], gh_ref[:W, 2 * FW :])
    gow = nt(g_ref[...], hid_ref[...]).astype(BF)
    gow = nn(pick, gow)
    bias = main_ref[NW : NW + OPAD, :]
    obias = jnp.broadcast_to(jnp.sum(obsum, axis=1, keepdims=True), (OPAD, W))

    lane = lax.broadcasted_iota(jnp.int32, (TAIL, W), 1)
    for k in range(3):
        lo, hi = k * TAIL, (k + 1) * TAIL
        tail = pltpu.roll(main_ref[MAIN:NW, :], 96 - 32 * k, 1)
        if hi <= MAIN:
            head = main_ref[lo:hi, :]
        else:
            head = jnp.concatenate(
                [main_ref[lo:MAIN, :], jnp.pad(gow, ((0, 0), (0, W - C)))], axis=0
            )
        out_ref[lo:hi, :] = jnp.where(lane < C, head, tail).astype(BF)
    ends = []
    for v in (bias, obias):
        top = v.astype(BF).astype(F32)
        ends += [top, v - top]
    out_ref[ROWS - 32 :, :] = jnp.concatenate(ends, axis=0).astype(BF)


def split_sums(total, is_last):
    out = total.astype(BF)
    start = total.shape[0] - 32
    fixed = []
    for at in (start, start + 16):
        whole = total[at : at + 8] + total[at + 8 : at + 16]
        top = whole.astype(BF).astype(F32)
        fixed += [top, whole - top]
    special = jnp.concatenate(([total[:start]] if start else []) + fixed, axis=0).astype(BF)
    return jnp.where(is_last, special, out)


def in_last():
    last = math.prod(lax.axis_size(a) for a in NEAR) - 1
    return flat_index(NEAR) == last ^ FIRST


def pass_on(value, pairs):
    outer, inner = (lax.axis_size(a) for a in DEPTH)
    place = [(d % inner) * outer + d // inner for d in range(outer * inner)]
    return lax.ppermute(value, DEPTH[::-1], [(place[i], place[j]) for i, j in pairs])


def plane_sum_kernel(in_ref, out_ref):
    total = in_ref[0].astype(F32)
    for k in range(1, in_ref.shape[0]):
        total = total + in_ref[k].astype(F32)
    out_ref[...] = split_sums(total, in_last())


def depth_sum_kernel(*refs):
    *in_refs, out_ref = refs
    total = in_refs[0][...].astype(F32)
    for ref in in_refs[1:]:
        total = total + ref[...].astype(F32)
    out_ref[...] = jnp.where(flat_index(DEPTH) < 2, split_sums(total, in_last()), jnp.zeros_like(out_ref))


def side_sum_kernel(part_ref, side_ref, out_ref):
    total = part_ref[...].astype(F32) + side_ref[...].astype(F32)
    at = flat_index(DEPTH)
    out_ref[...] = jnp.where((at == 2) | (at == 6), split_sums(total, in_last()), part_ref[...])


def copies_kernel(one_ref, two_ref, out_ref):
    either = one_ref[...] + two_ref[...]
    for k in range(out_ref.shape[0]):
        out_ref[k] = either


def unpack_kernel(in_ref, gw_ref, gb_ref, go_ref, gob_ref):
    def get(lo, hi):
        return in_ref[lo:hi, :].astype(F32)

    gw_ref[:MAIN, :] = get(0, MAIN)[:, :C]
    lane = lax.broadcasted_iota(jnp.int32, (TAIL, W), 1)
    tail = None
    for k in range(3):
        v = pltpu.roll(get(k * TAIL, (k + 1) * TAIL), 32 + 32 * k, 1)
        tail = v if tail is None else jnp.where(lane < 32 * k, tail, v)
    gw_ref[MAIN:, :] = tail[:, :C]
    gow = get(MAIN, MAIN + 96)
    for o in range(3):
        go_ref[o] = gow[o * 32 : o * 32 + TAPS, :C]
    sums = get(2016, 2048)
    gb_ref[...] = (sums[0:8] + sums[8:16])[0, :C]
    ob = sums[16:24] + sums[24:32]
    r8 = lax.broadcasted_iota(jnp.int32, (OPAD, W), 0)
    l8 = lax.broadcasted_iota(jnp.int32, (OPAD, W), 1)
    gob_ref[...] = jnp.sum(jnp.where(r8 == l8, ob, 0.0), axis=0)[:3]


VM = functools.partial(pl.BlockSpec, memory_space=pltpu.VMEM)
LIMIT = 48 * 1024 * 1024
SMALL = 4 * 1024 * 1024


def k1_call(n_rows, scale):
    return pl.pallas_call(
        functools.partial(device_kernel, n_rows, scale),
        out_shape=(
            jax.ShapeDtypeStruct((1, 3, F, 2, W), BF),
            jax.ShapeDtypeStruct((ROWS, W), BF),
        ),
        in_specs=[VM()] * 8,
        out_specs=(VM(), VM()),
        scratch_shapes=[
            pltpu.VMEM((KT + 16, POS), BF),
            pltpu.VMEM((F, 3 * C, FW), F32),
            pltpu.VMEM((C, POS), BF),
            pltpu.VMEM((C, POS), F32),
            pltpu.VMEM((GROWS, POS), F32),
            pltpu.VMEM((GROWS, POS), BF),
            pltpu.VMEM((2 * W, POS), BF),
            pltpu.VMEM((NW + 16, W), F32),
        ],
        compiler_params=pltpu.CompilerParams(vmem_limit_bytes=LIMIT),
        name="device_part",
    )


def local(latent_features, conv_weight, conv_bias, out_weight, out_bias, target_frames):
    sizes = [lax.axis_size(a) for a in EDGE_AXES]
    n_rows = math.prod(sizes)
    near = math.prod(lax.axis_size(a) for a in NEAR)
    clips = lax.axis_size("zh") * lax.axis_size("c")
    scale = 1.0 / math.sqrt(3 * clips * F * 2 * n_rows * W)

    own = jnp.transpose(latent_features[0], (1, 2, 0, 3))
    even = [(i, i ^ 1) for i in range(n_rows)]
    odd = [(i, ((i + 1) ^ 1) - 1) for i in range(1, n_rows - 1)]
    axes = EDGE_AXES + ("c",)
    one = lax.ppermute(own, axes, [(2 * i, 2 * j) for i, j in even] + [(2 * i + 1, 2 * j + 1) for i, j in odd])
    two = lax.ppermute(own, axes, [(2 * i, 2 * j) for i, j in odd] + [(2 * i + 1, 2 * j + 1) for i, j in even])

    wt = jnp.transpose(conv_weight.reshape(3, KT, C), (0, 2, 1)).reshape(3 * C, KT)
    wo = jnp.pad(jnp.transpose(out_weight, (2, 0, 1)), ((0, 0), (0, 5), (0, 0))).reshape(C, C)
    ob = jnp.pad(out_bias[:, None], ((0, 5), (0, 0)))
    tgt = jnp.pad(target_frames[0].reshape(3, F * 2 * W).astype(F32), ((0, 5), (0, 0)))

    decoded, packed = k1_call(n_rows, scale)(own, one, two, wt, conv_bias[:, None], wo, ob, tgt)

    chunk = ROWS // near

    def small(kernel, name, copies, *operands):
        return pl.pallas_call(
            kernel,
            out_shape=jax.ShapeDtypeStruct(copies + (chunk, W), BF),
            in_specs=[VM()] * len(operands),
            out_specs=VM(),
            compiler_params=pltpu.CompilerParams(vmem_limit_bytes=SMALL),
            name=name,
        )(*operands)

    parts = lax.all_to_all(packed.reshape(near, chunk, W), AXES, 0, 0, axis_index_groups=scatter_groups())
    part = small(plane_sum_kernel, "plane_sum", (), parts)
    side = pass_on(part, SIDE)
    more = small(side_sum_kernel, "side_sum", (), part, side)
    close = [pass_on(more, pairs) for pairs in CLOSE[::-1]]
    far = [pass_on(part, pairs) for pairs in FAR[::-1]]
    total = small(depth_sum_kernel, "depth_sum", (), part, *close, *far)
    received = [pass_on(total, pairs) for pairs in SPREAD[:-1]]
    total = sum(received, total)
    outer = pass_on(total, SPREAD[-1])
    parts = small(copies_kernel, "copies", (near,), total, outer)
    parts = lax.all_to_all(parts, AXES, 0, 0, axis_index_groups=scatter_groups())

    gw, gb, go, gob = pl.pallas_call(
        unpack_kernel,
        out_shape=(
            jax.ShapeDtypeStruct((NW, C), F32),
            jax.ShapeDtypeStruct((C,), F32),
            jax.ShapeDtypeStruct((3, TAPS, C), F32),
            jax.ShapeDtypeStruct((3,), F32),
        ),
        in_specs=[VM()],
        out_specs=(VM(),) * 4,
        compiler_params=pltpu.CompilerParams(vmem_limit_bytes=2 * SMALL),
        name="unpack",
    )(parts.reshape(ROWS, W))
    return (
        decoded,
        gw.reshape(TAPS, C, C),
        gb,
        jnp.transpose(go, (1, 2, 0)),
        gob,
    )


def solution(mesh):
    split = Mesh(mesh.devices.reshape(4, 2, 2, 4, 4, 2), AXES)
    frames = P(("zh", "c"), None, None, EDGE_AXES, None)
    return jax.shard_map(
        local,
        mesh=split,
        in_specs=(frames, P(), P(), P(), P(), frames),
        out_specs=(frames, P(), P(), P(), P()),
        check_vma=False,
    )
```
